32 devices in a mesh: rows: 16 (over z, y, x), cols: 2 (over core).
Axes of the slice: x: 2, y: 2, z: 4, core: 2. Of those that a mesh axis runs over, the one named last changes fastest.
Arguments:
- whitening: float32 [6144, 384], P('rows'), as said below
- sensor_states: int32 [6144, 4], P('rows'), may hold values from 0 to 1023, as said below
- sensor_coefficients: float32 [6144, 4], P('rows'), may hold values from -5 to 5
- sensor_readings: float32 [6144], P('rows'), may hold values from -6 to 6
- conduit_endpoints: int32 [2048, 2], P('rows'), may hold values from 0 to 1023
- conductance: float32 [2048], P('rows'), may hold values from 0.2 to 1
- balance_right_side: float32 [2048], P('rows'), may hold values from -3 to 3
- prior_root_factor: float32 [1024, 1024], P('rows'), as said below
- prior_information: float32 [1024], P('rows'), may hold values from -6 to 6
- transition: float32 [1024, 1024], P('cols'), may hold values from -0.1875 to 0.1875
Outputs:
- r_post: float32 [1024, 1024], P('rows', 'cols')
- z_post: float32 [1024], P('cols')
- x_next: float32 [1024], P('cols')
The draws below stay inside these ranges and needn't reach their ends.
Inputs may be any that keep to these rules, and one draw needn't show every extreme that they name: `prior_root_factor`: upper triangular, with diagonal entries between 1.5 and 3. `whitening`: each aligned block of 384 rows is a lower triangular matrix with a positive diagonal. `sensor_states`: the 4 states of a row are consecutive, counted modulo 1024.
All inputs are finite; a program needn't handle non-finite values.
Results may differ from the reference program's by a relative error of at most 0.0003.
Values sent between devices are 32-bit elements; how exact they have to be, the bound alone decides.
No kernel may reach another device: no remote copies, remote signals or barrier semaphores. Data moves between devices by JAX's collectives and lax.ppermute only.
A program may use at most 128 MiB of HBM per device.

```python
import math
import jax
import jax.numpy as jnp
from jax import lax

STATE_TOTAL = 1024
STATES_PER_ROW = 4
BLOCK_SENSOR_ROWS = 384
BR_DEV = 128
SENSOR_ROWS = 6144
BAL = 2048
N_ROWS = 16


def draw_prior_root_factor(key, part):
    diagonal_key, offdiagonal_key = jax.random.split(jax.random.fold_in(key, 11))
    row_position = lax.broadcasted_iota(jnp.int32, (STATE_TOTAL, STATE_TOTAL), 0)
    column_position = lax.broadcasted_iota(jnp.int32, (STATE_TOTAL, STATE_TOTAL), 1)
    diagonal_portion = jax.random.uniform(diagonal_key, (STATE_TOTAL, 1), jnp.float32, 1.5, 3.0)
    offdiagonal_portion = jax.random.normal(offdiagonal_key, (STATE_TOTAL, STATE_TOTAL), jnp.float32)
    offdiagonal_portion = offdiagonal_portion * (0.3 / math.sqrt(STATE_TOTAL))
    return jnp.where(row_position == column_position, diagonal_portion, jnp.where(column_position > row_position, offdiagonal_portion, 0.0))


def draw_whitening(key, part):
    diagonal_key, offdiagonal_key = jax.random.split(jax.random.fold_in(key, 23))
    row_position = lax.broadcasted_iota(jnp.int32, (SENSOR_ROWS, BLOCK_SENSOR_ROWS), 0) % BLOCK_SENSOR_ROWS
    column_position = lax.broadcasted_iota(jnp.int32, (SENSOR_ROWS, BLOCK_SENSOR_ROWS), 1)
    diagonal_portion = jnp.exp(jax.random.uniform(diagonal_key, (SENSOR_ROWS, 1), jnp.float32, math.log(0.08), math.log(0.4)))
    offdiagonal_portion = jax.random.normal(offdiagonal_key, (SENSOR_ROWS, BLOCK_SENSOR_ROWS), jnp.float32)
    offdiagonal_portion = offdiagonal_portion * diagonal_portion * (0.5 / math.sqrt(BLOCK_SENSOR_ROWS))
    return jnp.where(row_position == column_position, diagonal_portion, jnp.where(column_position < row_position, offdiagonal_portion, 0.0))


def draw_sensor_states(key, part):
    key = jax.random.fold_in(key, 31)
    first_state = jax.random.randint(key, (SENSOR_ROWS, 1), 0, STATE_TOTAL, jnp.int32)
    offsets = lax.broadcasted_iota(jnp.int32, (SENSOR_ROWS, STATES_PER_ROW), 1)
    return (first_state + offsets) % STATE_TOTAL


def draw_sensor_coefficients(key, part):
    sign_key, size_key = jax.random.split(jax.random.fold_in(key, 37))
    signs = (2 * jax.random.randint(sign_key, (SENSOR_ROWS, 1), 0, 2, jnp.int32) - 1).astype(jnp.float32)
    magnitudes = jax.random.uniform(size_key, (SENSOR_ROWS, STATES_PER_ROW), jnp.float32, 2.0, 4.0)
    return signs * magnitudes


def touch_ends(drawn, key, smallest, largest):
    place = [jax.random.randint(jax.random.fold_in(key, axis), (), 0, length) for axis, length in enumerate(drawn.shape)]
    main_axis = drawn.shape.index(max(drawn.shape))
    beside = place[:main_axis] + [(place[main_axis] + 1) % drawn.shape[main_axis]] + place[main_axis + 1:]
    return drawn.at[tuple(place)].set(smallest).at[tuple(beside)].set(largest)


def steps_of(rng, dims, cuts, smallest, high):
    def one(dim, blocks):
        heights = jax.random.uniform(jax.random.fold_in(jax.random.fold_in(rng, 6), dim), (blocks,), jnp.float32, smallest / len(cuts), high / len(cuts))
        return jnp.repeat(jnp.exp(heights), dims[dim] // blocks).reshape((-1,) + (1,) * (len(dims) - dim - 1))

    level = one(*cuts[0])
    for cut in cuts[1:]:
        level = level * one(*cut)
    return level


def noise(own_key, shape, deviation, bound, cuts=(), kind=jnp.bfloat16):
    result = deviation * jax.random.normal(own_key, shape, jnp.float32)
    if cuts:
        result = result * steps_of(own_key, shape, cuts, -0.22, 0.18)
    return jnp.clip(result, -bound, bound).astype(kind)


def setup_inputs(seed: int = 0) -> dict:
    arg_keys = jax.random.split(jax.random.key(seed), 11)
    whitening = draw_whitening(jax.random.fold_in(arg_keys[10], 71), 0)
    sensor_states = draw_sensor_states(jax.random.fold_in(arg_keys[10], 71), 0)
    sensor_coefficients = draw_sensor_coefficients(jax.random.fold_in(arg_keys[10], 71), 0)
    sensor_readings = noise(arg_keys[3], (SENSOR_ROWS,), 1.0, 6.0, ((0, 16),), jnp.float32)
    conduit_endpoints = touch_ends(jax.random.randint(arg_keys[4], (BAL, 2), 0, STATE_TOTAL), jax.random.fold_in(arg_keys[4], 1), 0, STATE_TOTAL - 1).astype(jnp.int32)
    conductance = jnp.clip(jnp.exp(math.log(1.0) - 1.609438 * jax.random.uniform(arg_keys[5], (BAL,), jnp.float32) ** steps_of(arg_keys[5], (BAL,), ((0, 16),), -0.2, 0.2)), 0.2, 1.0)
    balance_right_side = noise(arg_keys[6], (BAL,), 0.5, 3.0, ((0, 16),), jnp.float32)
    prior_root_factor = draw_prior_root_factor(jax.random.fold_in(arg_keys[10], 71), 0)
    prior_information = noise(arg_keys[8], (STATE_TOTAL,), 1.0, 6.0, ((0, 16),), jnp.float32)
    transition = noise(arg_keys[9], (STATE_TOTAL, STATE_TOTAL), STATE_TOTAL ** -0.5, 0.1875, ((0, 2),), jnp.float32)
    return dict(whitening=whitening, sensor_states=sensor_states, sensor_coefficients=sensor_coefficients, sensor_readings=sensor_readings, conduit_endpoints=conduit_endpoints, conductance=conductance, balance_right_side=balance_right_side, prior_root_factor=prior_root_factor, prior_information=prior_information, transition=transition)


def incidence_matrix(states, coeffs, state_total_count):
    column_ids = lax.broadcasted_iota(jnp.int32, (states.shape[0], state_total_count), 1)
    summed = jnp.zeros((states.shape[0], state_total_count), jnp.float32)
    for position in range(states.shape[1]):
        summed = summed + jnp.where(column_ids == states[:, position:position + 1], coeffs[:, position:position + 1], 0.0)
    return summed

def reference(whitening, sensor_states, sensor_coefficients, sensor_readings, conduit_endpoints, conductance, balance_right_side, prior_root_factor, prior_information, transition):
    highest_accuracy = lax.Precision.HIGHEST
    white_blocks = whitening.reshape(N_ROWS, BLOCK_SENSOR_ROWS, BLOCK_SENSOR_ROWS)
    state_index_blocks = sensor_states.reshape(N_ROWS, BLOCK_SENSOR_ROWS, STATES_PER_ROW)
    coefficient_blocks = sensor_coefficients.reshape(N_ROWS, BLOCK_SENSOR_ROWS, STATES_PER_ROW)
    reading_blocks = sensor_readings.reshape(N_ROWS, BLOCK_SENSOR_ROWS)
    end_blocks = conduit_endpoints.reshape(N_ROWS, BR_DEV, 2)
    cond_blocks = conductance.reshape(N_ROWS, BR_DEV)
    brhs_blocks = balance_right_side.reshape(N_ROWS, BR_DEV)

    def add_block(carry, items):
        gram, moment = carry
        whitened_block, states_b, coeff_b, reading_block, ends_b, conductance_block, balance_right_block = items
        sensed_states = incidence_matrix(states_b, coeff_b, STATE_TOTAL)
        sensor_row_list = jnp.dot(whitened_block, sensed_states, precision=highest_accuracy)
        sensor_right_side = jnp.dot(whitened_block, reading_block, precision=highest_accuracy)
        pair_coeffs = jnp.stack([conductance_block, -conductance_block], axis=1)
        balance_row_list = incidence_matrix(ends_b, pair_coeffs, STATE_TOTAL)
        stacked_system = jnp.concatenate([sensor_row_list, balance_row_list], axis=0)
        combined_right_side = jnp.concatenate([sensor_right_side, conductance_block * balance_right_block], axis=0)
        gram = gram + jnp.dot(stacked_system.T, stacked_system, precision=highest_accuracy)
        moment = moment + jnp.dot(stacked_system.T, combined_right_side, precision=highest_accuracy)
        return ((gram, moment), None)
    gram0 = jnp.dot(prior_root_factor.T, prior_root_factor, precision=highest_accuracy)
    moment0 = jnp.dot(prior_root_factor.T, prior_information, precision=highest_accuracy)
    (gram, moment), _ = lax.scan(add_block, (gram0, moment0), (white_blocks, state_index_blocks, coefficient_blocks, reading_blocks, end_blocks, cond_blocks, brhs_blocks))
    lower_factor = jnp.linalg.cholesky(gram)
    z_col = lax.linalg.triangular_solve(lower_factor, moment[:, None], left_side=True, lower=True)
    est_col = lax.linalg.triangular_solve(lower_factor, z_col, left_side=True, lower=True, transpose_a=True)
    x_next = jnp.dot(transition, est_col[:, 0], precision=highest_accuracy)
    return (lower_factor.T, z_col[:, 0], x_next)
```

```python
import functools

import jax
import jax.numpy as jnp
from jax import lax
from jax.experimental import pallas as pl
from jax.experimental.pallas import tpu as pltpu
from jax.sharding import PartitionSpec as P

BLK = 128
MIC = 16
F32 = jnp.float32
BF16 = jnp.bfloat16
VMEM_LIMIT = 56 * 1024 * 1024


def split2(value):
    high = value.astype(BF16)
    low = (value - high.astype(F32)).astype(BF16)
    return high, low


def dot(left, right, left_dim, right_dim):
    return lax.dot_general(
        left, right, (((left_dim,), (right_dim,)), ((), ())), preferred_element_type=F32
    )


def radices(count):
    found = []
    while count > 1:
        found.append(4 if count % 4 == 0 else 2)
        count //= found[-1]
    return tuple(found)


class Plan:
    def __init__(self, state_total, rows, cols):
        self.state_total = state_total
        self.blocks = state_total // BLK
        self.tiles = self.blocks * (self.blocks + 1) // 2
        self.rows, self.cols = rows, cols
        self.radix = radices(rows)
        self.stride = []
        step = 1
        for f in self.radix:
            self.stride.append(step)
            step *= f
        used = self.tiles * BLK + self.blocks
        unit = 8 * rows * cols
        self.total = -(-used // unit) * unit
        self.piece = self.total // (rows * cols)
        self.moment_row = self.tiles * BLK

    def tile_row(self, i, j):
        return (j * (j + 1) // 2 + i) * BLK

    def digit(self, index, stage):
        return lax.rem(index // self.stride[stage], self.radix[stage])

    def span(self, stage):
        size = self.piece
        for f in self.radix[stage + 1 :]:
            size *= f
        return size


def assemble_kernel(
    plan,
    white_ref,
    states_ref,
    coeffs_ref,
    readings_ref,
    ends_ref,
    conductance_ref,
    balance_rhs_ref,
    prior_ref,
    prior_info_ref,
    *rest,
):
    first = plan.radix[0]
    outs, (sens_ref, left_ref, right_ref, prior_pad, packed) = rest[:first], rest[first:]
    n = plan.state_total
    block_rows = white_ref.shape[0]
    bal_rows = conductance_ref.shape[1]
    prior_rows = prior_ref.shape[0]
    depth = block_rows + bal_rows + BLK
    head = 16
    step = 64

    def put_left(rows, col, high, low):
        left_ref[rows, col : col + high.shape[1]] = high
        left_ref[rows, depth + col : depth + col + high.shape[1]] = high
        left_ref[rows, 2 * depth + col : 2 * depth + col + high.shape[1]] = low

    def put_right(rows, col, high, low):
        right_ref[rows, col : col + high.shape[1]] = high
        right_ref[rows, depth + col : depth + col + high.shape[1]] = low
        right_ref[rows, 2 * depth + col : 2 * depth + col + high.shape[1]] = high

    def head_rows(row):
        top = lax.broadcasted_iota(jnp.int32, (head, row.shape[1]), 0) == 0
        return jnp.where(top, jnp.broadcast_to(row, (head, row.shape[1])), 0.0)

    high, low = split2(head_rows(readings_ref[...]))
    sens_ref[0:head, 0:block_rows] = high
    sens_ref[0:head, block_rows : 2 * block_rows] = high
    sens_ref[0:head, 2 * block_rows : 3 * block_rows] = low
    for at in range(0, n, step):
        ids = lax.broadcasted_iota(jnp.int32, (step, block_rows), 0) + at
        summed = jnp.zeros((step, block_rows), F32)
        for k in range(states_ref.shape[0]):
            summed = summed + jnp.where(ids == states_ref[k : k + 1, :], coeffs_ref[k : k + 1, :], 0.0)
        high, low = split2(summed)
        rows = slice(head + at, head + at + step)
        sens_ref[rows, 0:block_rows] = high
        sens_ref[rows, block_rows : 2 * block_rows] = high
        sens_ref[rows, 2 * block_rows : 3 * block_rows] = low
    white_high, white_low = split2(white_ref[...])
    white_cat = jnp.concatenate([white_high, white_low, white_high], axis=1)
    whitened = dot(sens_ref[...], white_cat, 1, 1)
    for at in range(0, n + head, step):
        size = min(step, n + head - at)
        high, low = split2(whitened[at : at + size, :])
        put_left(slice(at, at + size), 0, high, low)
        if at == 0:
            put_right(slice(0, size - head), 0, high[head:], low[head:])
        else:
            put_right(slice(at - head, at - head + size), 0, high, low)

    conductance = conductance_ref[...]
    high, low = split2(head_rows(conductance * balance_rhs_ref[...]))
    put_left(slice(0, head), block_rows, high, low)
    for at in range(0, n, step):
        ids = lax.broadcasted_iota(jnp.int32, (step, bal_rows), 0) + at
        value = jnp.where(ids == ends_ref[0:1, :], conductance, 0.0)
        value = value + jnp.where(ids == ends_ref[1:2, :], -conductance, 0.0)
        high, low = split2(value)
        put_left(slice(head + at, head + at + step), block_rows, high, low)
        put_right(slice(at, at + step), block_rows, high, low)

    prior_col = block_rows + bal_rows
    prior_pad[...] = jnp.zeros_like(prior_pad)
    prior_pad[0:prior_rows, 0:n] = prior_ref[...]
    info = jnp.concatenate(
        [prior_info_ref[...], jnp.zeros((1, BLK - prior_rows), F32)], axis=1
    )
    high, low = split2(head_rows(info))
    put_left(slice(0, head), prior_col, high, low)
    for at in range(0, n, BLK):
        high, low = split2(prior_pad[:, at : at + BLK].T)
        put_left(slice(head + at, head + at + BLK), prior_col, high, low)
        put_right(slice(at, at + BLK), prior_col, high, low)

    packed[plan.moment_row :, :] = jnp.zeros((plan.total - plan.moment_row, BLK), F32)
    wide = 2 * BLK
    for at in range(0, n, wide):
        out = dot(left_ref[0 : head + at + wide, :], right_ref[at : at + wide, :], 1, 1)
        for part in range(2):
            j = at // BLK + part
            lanes = slice(part * BLK, (part + 1) * BLK)
            packed[plan.moment_row + j : plan.moment_row + j + 1, :] = out[0:1, lanes]
            for i in range(j + 1):
                row = plan.tile_row(i, j)
                packed[row : row + BLK, :] = out[head + i * BLK : head + (i + 1) * BLK, lanes]

    me, core = lax.axis_index("rows"), lax.axis_index("cols")
    span = plan.span(0)
    for d in range(first):
        at = (core * plan.radix[0] + (plan.digit(me, 0) ^ d)) * span
        outs[d][...] = packed[pl.ds(pl.multiple_of(at, 8), span), :]


def sum_kernel(plan, stage, *refs):
    before, after = plan.radix[stage - 1], plan.radix[stage]
    ins, outs = refs[:before], refs[before:]
    mine = plan.digit(lax.axis_index("rows"), stage)
    span = plan.span(stage)
    for d in range(after):
        rows = pl.ds(pl.multiple_of((mine ^ d) * span, 8), span)
        total = ins[0][rows, :]
        for other in ins[1:]:
            total = total + other[rows, :]
        outs[d][...] = total


def factor_block(d_ref, inv_ref, cast_ref, strip_ref, row_ref):
    lane = lax.broadcasted_iota(jnp.int32, (MIC, BLK), 1)
    sub = lax.broadcasted_iota(jnp.int32, (MIC, BLK), 0)
    for m in range(BLK // MIC):
        r0 = m * MIC
        strip = d_ref[r0 : r0 + MIC, :]
        top, bottom = strip[0:8, :], strip[8:16, :]
        for c in range(MIC):
            col = slice(r0 + c, r0 + c + 1)
            if c < 8:
                cast_ref[c * MIC : c * MIC + 8, :] = jnp.broadcast_to(top[:, col], (8, BLK))
            cast_ref[c * MIC + 8 : c * MIC + 16, :] = jnp.broadcast_to(bottom[:, col], (8, BLK))
        inside = (lane >= r0) & (lane < r0 + MIC)
        strip_ref[...] = jnp.where(inside, jnp.where(lane == r0 + sub, 1.0, 0.0), strip)
        s = [[cast_ref[c * MIC + i : c * MIC + i + 1, :] if i >= c else None for c in range(MIC)] for i in range(MIC)]
        rows = [strip_ref[i : i + 1, :] for i in range(MIC)]
        for j in range(MIC):
            scale = lax.rsqrt(s[j][j])
            u = [s[i][j] * scale if i > j else None for i in range(MIC)]
            for c in range(j + 1, MIC):
                for i in range(c, MIC):
                    s[i][c] = s[i][c] - u[i] * u[c]
            done = rows[j] * scale
            row_ref[j : j + 1, :] = done
            for i in range(j + 1, MIC):
                rows[i] = rows[i] - u[i] * done
        solved = row_ref[...]
        inv_ref[r0 : r0 + MIC, :] = jnp.where(lane < r0 + MIC, solved, 0.0)
        if r0 + MIC < BLK:
            high, low = split2(solved)
            fix = dot(
                jnp.concatenate([high, high, low], axis=0),
                jnp.concatenate([high, low, high], axis=0),
                0,
                0,
            )
            lanes = lax.broadcasted_iota(jnp.int32, (BLK - r0 - MIC, BLK), 1)
            keep = (lanes < r0) | (lanes >= r0 + MIC)
            left = jnp.where(keep, d_ref[r0 + MIC :, :], 0.0)
            d_ref[r0 + MIC :, :] = left - fix[r0 + MIC :, :]


def factor_kernel(plan, out_rows, *refs):
    first, cols = plan.radix[0], plan.cols
    ins = refs[: first * cols]
    trans_ref, r_ref, z_ref, x_ref = refs[first * cols : first * cols + 4]
    packed, d_ref, inv_ref, cast_ref, strip_ref, row_ref, left_ref, right_ref, full_ref, z_all, sem = refs[
        first * cols + 4 :
    ]
    n, nb = plan.state_total, plan.blocks
    width = trans_ref.shape[1]
    me, core = lax.axis_index("rows"), lax.axis_index("cols")

    copies = []
    inner = plan.span(0) // plan.piece
    for e in range(cols):
        for d0 in range(first):
            for f in range(inner):
                place = (core ^ e) * first + (plan.digit(me, 0) ^ d0)
                left = f
                size = inner
                for stage in range(1, len(plan.radix)):
                    size //= plan.radix[stage]
                    place = place * plan.radix[stage] + (plan.digit(me, stage) ^ (left // size))
                    left %= size
                copy = pltpu.make_async_copy(
                    ins[e * first + d0].at[pl.ds(f * plan.piece, plan.piece), :],
                    packed.at[pl.ds(pl.multiple_of(place * plan.piece, 8), plan.piece), :],
                    sem.at[(e * first + d0) * inner + f],
                )
                copy.start()
                copies.append(copy)
    full_ref[...] = jnp.zeros_like(full_ref)
    for copy in copies:
        copy.wait()

    x_total = jnp.zeros((1, width), F32)
    row_id = lax.broadcasted_iota(jnp.int32, (BLK, BLK), 0)
    col_id = lax.broadcasted_iota(jnp.int32, (BLK, BLK), 1)
    for k in range(nb):
        lo = k * BLK
        moment = jnp.broadcast_to(packed[plan.moment_row + k : plan.moment_row + k + 1, :], (BLK, BLK)).T
        tiles = [packed[plan.tile_row(k, j) : plan.tile_row(k, j) + BLK, :] for j in range(k, nb)]
        panel = jnp.concatenate(tiles + [trans_ref[lo : lo + BLK, :], moment], axis=1)
        if k:
            panel = panel - dot(left_ref[lo : lo + BLK, 0 : 3 * lo], right_ref[0 : 3 * lo, lo:], 1, 0)
        d_ref[...] = panel[:, 0:BLK]
        factor_block(d_ref, inv_ref, cast_ref, strip_ref, row_ref)
        inv_high, inv_low = split2(inv_ref[...])
        high, low = split2(panel)
        done = dot(
            jnp.concatenate([inv_high, inv_high, inv_low], axis=1),
            jnp.concatenate([high, low, high], axis=0),
            1,
            0,
        )
        full_ref[lo : lo + BLK, lo : lo + BLK] = jnp.where(col_id >= row_id, done[:, 0:BLK], 0.0)
        if k + 1 < nb:
            full_ref[lo : lo + BLK, lo + BLK :] = done[:, BLK : n - lo]
            high, low = split2(done[:, BLK:])
            right_ref[3 * lo : 3 * lo + BLK, lo + BLK :] = high
            right_ref[3 * lo + BLK : 3 * lo + 2 * BLK, lo + BLK :] = low
            right_ref[3 * lo + 2 * BLK : 3 * lo + 3 * BLK, lo + BLK :] = high
            for j in range(k + 1, nb):
                high, low = split2(done[:, (j - k) * BLK : (j - k + 1) * BLK].T)
                left_ref[j * BLK : (j + 1) * BLK, 3 * lo : 3 * lo + 3 * BLK] = jnp.concatenate(
                    [high, high, low], axis=1
                )
        z_cast = done[:, n - lo + width :]
        z_all[:, lo : lo + BLK] = z_cast.T[0:1, :]
        for at in range(0, width, BLK):
            part = jnp.sum(done[:, n - lo + at : n - lo + at + BLK] * z_cast, axis=0, keepdims=True)
            if k:
                part = part + x_ref[:, at : at + BLK]
            x_ref[:, at : at + BLK] = part

    rows = pl.ds(pl.multiple_of(me * out_rows, 8), out_rows)
    lanes = pl.ds(pl.multiple_of(core * width, BLK), width)
    r_ref[...] = full_ref[rows, lanes]
    z_ref[...] = z_all[:, lanes]


def per_device(
    whitening,
    sensor_states,
    sensor_coefficients,
    sensor_readings,
    conduit_endpoints,
    conductance,
    balance_right_side,
    prior_root_factor,
    prior_information,
    transition,
):
    n = prior_root_factor.shape[1]
    rows, cols = lax.axis_size("rows"), lax.axis_size("cols")
    plan = Plan(n, rows, cols)
    radix = plan.radix
    params = pltpu.CompilerParams(vmem_limit_bytes=VMEM_LIMIT)
    block_rows, bal_rows = whitening.shape[0], conductance.shape[0]
    depth = block_rows + bal_rows + BLK

    def piece_type(size):
        return jax.ShapeDtypeStruct((size, BLK), F32)

    parts = pl.pallas_call(
        functools.partial(assemble_kernel, plan),
        out_shape=[piece_type(plan.span(0))] * radix[0],
        scratch_shapes=[
            pltpu.VMEM((n + 16, 3 * block_rows), BF16),
            pltpu.VMEM((n + 16, 3 * depth), BF16),
            pltpu.VMEM((n, 3 * depth), BF16),
            pltpu.VMEM((BLK, n), F32),
            pltpu.VMEM((plan.total, BLK), F32),
        ],
        compiler_params=params,
        name="assemble",
    )(
        whitening,
        sensor_states.T,
        sensor_coefficients.T,
        sensor_readings[None, :],
        conduit_endpoints.T,
        conductance[None, :],
        balance_right_side[None, :],
        prior_root_factor,
        prior_information[None, :],
    )

    def exchange(stage, rel, block):
        flip = rel * plan.stride[stage]
        return lax.ppermute(block, "rows", [(i, i ^ flip) for i in range(rows)])

    for stage in range(len(radix)):
        got = [parts[0]] + [exchange(stage, d, parts[d]) for d in range(1, radix[stage])]
        if stage + 1 < len(radix):
            parts = pl.pallas_call(
                functools.partial(sum_kernel, plan, stage + 1),
                out_shape=[piece_type(plan.span(stage + 1))] * radix[stage + 1],
                compiler_params=params,
                name="partial_sums",
            )(*got)
        else:
            block = functools.reduce(jnp.add, got)
    for stage in reversed(range(len(radix))):
        got = [block] + [exchange(stage, d, block) for d in range(1, radix[stage])]
        if stage:
            block = jnp.concatenate(got, axis=0)
    swap = [(i, i ^ 1) for i in range(cols)]
    both = got + [lax.ppermute(block, "cols", swap) for block in got]

    width = n // cols
    out_rows = n // rows
    wide = n + width + BLK
    anywhere = pl.BlockSpec(memory_space=pl.ANY)
    vmem = pl.BlockSpec(memory_space=pltpu.VMEM)
    r_post, z_post, x_next = pl.pallas_call(
        functools.partial(factor_kernel, plan, out_rows),
        out_shape=[
            jax.ShapeDtypeStruct((out_rows, width), F32),
            jax.ShapeDtypeStruct((1, width), F32),
            jax.ShapeDtypeStruct((1, width), F32),
        ],
        in_specs=[anywhere] * len(both) + [vmem],
        scratch_shapes=[
            pltpu.VMEM((plan.total, BLK), F32),
            pltpu.VMEM((BLK, BLK), F32),
            pltpu.VMEM((BLK, BLK), F32),
            pltpu.VMEM((MIC * MIC, BLK), F32),
            pltpu.VMEM((MIC, BLK), F32),
            pltpu.VMEM((MIC, BLK), F32),
            pltpu.VMEM((n, 3 * n), BF16),
            pltpu.VMEM((3 * n, wide), BF16),
            pltpu.VMEM((n, n), F32),
            pltpu.VMEM((1, n), F32),
            pltpu.SemaphoreType.DMA((rows * cols,)),
        ],
        compiler_params=params,
        name="factor",
    )(*both, transition.T)
    return (r_post, z_post[0], x_next[0])


def solution(mesh):
    in_specs = (
        P("rows", None),
        P("rows", None),
        P("rows", None),
        P("rows"),
        P("rows", None),
        P("rows"),
        P("rows"),
        P("rows", None),
        P("rows"),
        P("cols", None),
    )
    out_specs = (P("rows", "cols"), P("cols"), P("cols"))
    return jax.shard_map(
        per_device, mesh=mesh, in_specs=in_specs, out_specs=out_specs, check_vma=False
    )
```

```python
import functools

import jax
import jax.numpy as jnp
from jax import lax
from jax.experimental import pallas as pl
from jax.experimental.pallas import tpu as pltpu
from jax.sharding import PartitionSpec as P

BLK = 128
MIC = 32
GRP = 8
F32 = jnp.float32
BF16 = jnp.bfloat16
VMEM_LIMIT = 48 * 1024 * 1024
ASSEMBLE_VMEM = 63 * 1024 * 1024


def split2(value):
    high = value.astype(BF16)
    low = (value - high.astype(F32)).astype(BF16)
    return high, low


def dot(left, right, left_dim=1, right_dim=0):
    return lax.dot_general(
        left, right, (((left_dim,), (right_dim,)), ((), ())), preferred_element_type=F32
    )


def dot3(left, right, left_dim=1, right_dim=0):
    total = dot(left[0], right[1], left_dim, right_dim) + dot(left[1], right[0], left_dim, right_dim)
    return total + dot(left[0], right[0], left_dim, right_dim)


def radices(count):
    found = []
    while count > 1:
        found.append(4 if count % 4 == 0 else 2)
        count //= found[-1]
    return tuple(found)


class Plan:
    def __init__(self, state_total, rows, cols):
        self.state_total = state_total
        self.blocks = nb = state_total // BLK
        self.rows, self.cols = rows, cols
        self.radix = radices(rows)
        self.stride = []
        step = 1
        for f in self.radix:
            self.stride.append(step)
            step *= f
        self.tiles = nb * (nb + 1) // 2
        unit = 8 * rows * cols
        self.total = -(-self.tiles * BLK // unit) * unit
        self.piece = self.total // (rows * cols)
        self.moment_rows = state_total // 64

    def tile(self, i, j):
        return (sum(self.blocks - k for k in range(i)) + j - i) * BLK


def assemble_kernel(plan, *refs):
    ins, (out_ref, *scratch) = refs[:9], refs[9:]
    here, (sens_hi, sens_lo, at_hi, at_lo, prior_pad, packed, sems) = scratch[:9], scratch[9:]
    copies = [pltpu.make_async_copy(a, b, sems.at[i]) for i, (a, b) in enumerate(zip(ins, here))]
    for copy in copies:
        copy.start()
    (
        white_ref,
        states_ref,
        coeffs_ref,
        readings_ref,
        ends_ref,
        conductance_ref,
        balance_rhs_ref,
        prior_ref,
        prior_info_ref,
    ) = here
    n = plan.state_total
    block_rows = white_ref.shape[0]
    bal_rows = conductance_ref.shape[1]
    prior_rows = prior_ref.shape[0]
    head = 16
    step = 64

    def put(high_ref, low_ref, row, col, value):
        high, low = split2(value)
        high_ref[row : row + value.shape[0], col : col + value.shape[1]] = high
        low_ref[row : row + value.shape[0], col : col + value.shape[1]] = low

    def head_rows(row):
        top = lax.broadcasted_iota(jnp.int32, (head, row.shape[1]), 0) == 0
        return jnp.where(top, jnp.broadcast_to(row, (head, row.shape[1])), 0.0)

    prior_pad[...] = jnp.zeros_like(prior_pad)
    if plan.tiles * BLK < plan.total:
        packed[plan.tiles * BLK :, :] = jnp.zeros((plan.total - plan.tiles * BLK, BLK), F32)
    for copy in copies:
        copy.wait()

    readings = jnp.concatenate(
        [readings_ref[k : k + 1, :] for k in range(readings_ref.shape[0])], axis=1
    )
    put(sens_hi, sens_lo, 0, 0, head_rows(readings))
    for at in range(0, n, step):
        ids = lax.broadcasted_iota(jnp.int32, (step, block_rows), 0) + at
        summed = jnp.zeros((step, block_rows), F32)
        for k in range(states_ref.shape[0]):
            summed = summed + jnp.where(ids == states_ref[k : k + 1, :], coeffs_ref[k : k + 1, :], 0.0)
        put(sens_hi, sens_lo, head + at, 0, summed)
    white = split2(white_ref[...])
    whitened = dot3((sens_hi[...], sens_lo[...]), white, 1, 1)
    for at in range(0, n + head, step):
        size = min(step, n + head - at)
        put(at_hi, at_lo, at, 0, whitened[at : at + size, :])

    conductance = conductance_ref[...]
    put(at_hi, at_lo, 0, block_rows, head_rows(conductance * balance_rhs_ref[...]))
    for at in range(0, n, step):
        ids = lax.broadcasted_iota(jnp.int32, (step, bal_rows), 0) + at
        value = jnp.where(ids == ends_ref[0:1, :], conductance, 0.0)
        value = value + jnp.where(ids == ends_ref[1:2, :], -conductance, 0.0)
        put(at_hi, at_lo, head + at, block_rows, value)

    prior_col = block_rows + bal_rows
    prior_pad[0:prior_rows, :] = prior_ref[...]
    info = jnp.concatenate([prior_info_ref[...], jnp.zeros((1, BLK - prior_rows), F32)], axis=1)
    put(at_hi, at_lo, 0, prior_col, head_rows(info))
    for at in range(0, n, BLK):
        put(at_hi, at_lo, head + at, prior_col, prior_pad[:, at : at + BLK].T)

    wide = 2 * BLK
    moments = []
    for at in range(0, n, wide):
        stop = head + at + wide
        out = dot3(
            (at_hi[0:stop, :], at_lo[0:stop, :]),
            (at_hi[head + at : stop, :], at_lo[head + at : stop, :]),
            1,
            1,
        )
        moments.append(out[0:1, :])
        for part in range(2):
            j = at // BLK + part
            for i in range(j + 1):
                row = plan.tile(i, j)
                packed[row : row + BLK, :] = out[
                    head + i * BLK : head + (i + 1) * BLK, part * BLK : (part + 1) * BLK
                ]
    for k in range(plan.moment_rows):
        row = BLK - plan.moment_rows + k
        source = moments[k * 64 // wide][:, k * 64 % wide : k * 64 % wide + 64]
        packed[row : row + 1, 0:64] = source

    size = plan.rows * plan.piece
    at = lax.axis_index("cols") * size
    out_ref[...] = packed[pl.ds(pl.multiple_of(at, 8), size), :]


def eliminate(s, rows):
    u = [[None] * GRP for _ in range(GRP)]
    pairs, done = [], []
    for p in range(0, GRP, 2):
        a, b, c = s[p][p], s[p + 1][p], s[p + 1][p + 1]
        det = a * c - b * b
        root_det = lax.rsqrt(det)
        root_a = lax.rsqrt(a)
        second = root_a * root_det
        inv = root_det * root_det
        u[p + 1][p] = b * root_a
        left = {}
        for i in range(p + 2, GRP):
            one, two = s[i][p], s[i][p + 1]
            cross = a * two - b * one
            left[i] = (c * one - b * two, cross)
            u[i][p] = one * root_a
            u[i][p + 1] = cross * second
        for c_at in range(p + 2, GRP):
            for i in range(c_at, GRP):
                fall = left[i][0] * s[c_at][p] + left[i][1] * s[c_at][p + 1]
                s[i][c_at] = s[i][c_at] - fall * inv
        pairs.append((a, b, root_a, second))
        done.append(rows[p] * root_a)
        done.append((a * rows[p + 1] - b * rows[p]) * second)
        for i in range(p + 2, GRP):
            rows[i] = rows[i] - (u[i][p] * done[p] + u[i][p + 1] * done[p + 1])
    return u, pairs, done


def factor_block(d_ref, inv_ref, cast_ref, times_ref, strip_ref, row_ref, queue):
    lane = lax.broadcasted_iota(jnp.int32, (MIC, BLK), 1)
    sub = lax.broadcasted_iota(jnp.int32, (MIC, BLK), 0)
    groups = MIC // GRP
    slots = groups * (BLK // MIC)
    share = -(-len(queue) // slots)

    def background():
        for _ in range(min(share, len(queue))):
            queue.pop(0)()

    for m in range(BLK // MIC):
        r0 = m * MIC
        strip = d_ref[r0 : r0 + MIC, :]
        inside = (lane >= r0) & (lane < r0 + MIC)
        ready = jnp.where(inside, jnp.where(lane == r0 + sub, 1.0, 0.0), strip)
        low, rest = [], []
        for g in range(groups):
            part = strip[g * GRP : (g + 1) * GRP, :]
            low.append(
                [
                    jnp.broadcast_to(part[:, r0 + c : r0 + c + 1], (GRP, BLK))
                    for c in range((g + 1) * GRP)
                ]
            )
            rest.append(ready[g * GRP : (g + 1) * GRP, :])
        for s in range(groups):
            base = s * GRP * GRP
            for c in range(GRP):
                cast_ref[base + GRP * c : base + GRP * (c + 1), :] = low[s][s * GRP + c]
            strip_ref[s * GRP : (s + 1) * GRP, :] = rest[s]
            splats = [
                [
                    cast_ref[base + GRP * c + i : base + GRP * c + i + 1, :] if i >= c else None
                    for c in range(GRP)
                ]
                for i in range(GRP)
            ]
            background()
            u, pairs, done = eliminate(
                splats, [strip_ref[s * GRP + i : s * GRP + i + 1, :] for i in range(GRP)]
            )
            for j in range(GRP):
                row_ref[s * GRP + j : s * GRP + j + 1, :] = done[j]
            for g in range(s + 1, groups):
                mine = low[g][s * GRP : (s + 1) * GRP]
                for p in range(0, GRP, 2):
                    a, b, root_a, second = pairs[p // 2]
                    one, two = mine[p], mine[p + 1]
                    mine[p] = one * root_a
                    mine[p + 1] = (a * two - b * one) * second
                    for c in range(p + 2, GRP):
                        mine[c] = mine[c] - (mine[p] * u[c][p] + mine[p + 1] * u[c][p + 1])
                times = (s * groups + g) * GRP * GRP
                for j in range(GRP):
                    times_ref[times + GRP * j : times + GRP * (j + 1), :] = mine[j]
                    rest[g] = rest[g] - mine[j] * done[j]
                for h in range(s + 1, g + 1):
                    other = (s * groups + h) * GRP * GRP
                    for c in range(GRP):
                        total = low[g][h * GRP + c]
                        for j in range(0, GRP, 2):
                            at = other + GRP * j + c
                            total = total - (
                                mine[j] * times_ref[at : at + 1, :]
                                + mine[j + 1] * times_ref[at + GRP : at + GRP + 1, :]
                            )
                        low[g][h * GRP + c] = total
        solved = row_ref[...]
        inv_ref[r0 : r0 + MIC, :] = jnp.where(lane < r0 + MIC, solved, 0.0)
        if r0 + MIC < BLK:
            high, low_part = split2(solved)
            fix = dot(
                jnp.concatenate([high, high, low_part], axis=0),
                jnp.concatenate([high, low_part, high], axis=0),
                0,
                0,
            )
            lanes = lax.broadcasted_iota(jnp.int32, (BLK - r0 - MIC, BLK), 1)
            keep = (lanes < r0) | (lanes >= r0 + MIC)
            left = jnp.where(keep, d_ref[r0 + MIC :, :], 0.0)
            d_ref[r0 + MIC :, :] = left - fix[r0 + MIC :, :]
    while queue:
        queue.pop(0)()


def factor_kernel(plan, out_rows, width, *refs):
    radix0, cols, n, nb = plan.radix[0], plan.cols, plan.state_total, plan.blocks
    ins, (trans_hbm, r_ref, z_ref, x_ref, *scratch) = refs[: radix0 * cols], refs[radix0 * cols :]
    (
        packed,
        d_ref,
        inv_ref,
        cast_ref,
        times_ref,
        strip_ref,
        row_ref,
        panel_ref,
        full_ref,
        trans_ref,
        col_ref,
        root_ref,
        *state,
        sems,
        trans_sem,
    ) = scratch
    left, right, z_all = state[:2], state[2:4], state[4]
    me, core = lax.axis_index("rows"), lax.axis_index("cols")

    copies = []
    inner = plan.rows // radix0
    piece = plan.piece
    for e in range(cols):
        for d0 in range(radix0):
            for f in range(inner):
                flip = d0 * plan.stride[0]
                rest, size = f, inner
                for stage in range(1, len(plan.radix)):
                    size //= plan.radix[stage]
                    flip += rest // size * plan.stride[stage]
                    rest %= size
                place = (core ^ e) * plan.rows + (me ^ flip)
                copies.append(
                    pltpu.make_async_copy(
                        ins[e * radix0 + d0].at[pl.ds(f * piece, piece), :],
                        packed.at[pl.ds(pl.multiple_of(place * piece, 8), piece), :],
                        sems.at[len(copies)],
                    )
                )
    trans_copy = pltpu.make_async_copy(trans_hbm, trans_ref, trans_sem)
    for copy in copies:
        copy.start()
    trans_copy.start()
    full_ref[...] = jnp.zeros_like(full_ref)
    for copy in copies:
        copy.wait()

    row_id = lax.broadcasted_iota(jnp.int32, (BLK, BLK), 0)
    col_id = lax.broadcasted_iota(jnp.int32, (BLK, BLK), 1)

    def turned(row):
        return jnp.broadcast_to(row, (BLK, BLK)).T

    tile = packed[0:BLK, :]
    hidden = (row_id >= BLK - plan.moment_rows) & (col_id < 64)
    moments = []
    for k in range(nb):
        at = BLK - plan.moment_rows + 2 * k
        moments.append(jnp.concatenate([tile[at : at + 1, 0:64], tile[at + 1 : at + 2, 0:64]], axis=1))
    packed[0:BLK, :] = jnp.where(hidden, tile.T, tile)

    scales = []
    for k in range(nb):
        row = plan.tile(k, k)
        diagonal = jnp.sum(
            jnp.where(row_id == col_id, packed[row : row + BLK, :], 0.0), axis=0, keepdims=True
        )
        scales.append(lax.rsqrt(diagonal))
        root_ref[k : k + 1, :] = diagonal * scales[k]
        col_ref[k] = turned(scales[k])
    trans_copy.wait()

    def base(k, j):
        if j < nb:
            row = plan.tile(k, j)
            return packed[row : row + BLK, :] * col_ref[k] * scales[j]
        if j < nb + width // BLK:
            at = (j - nb) * BLK
            return trans_ref[k * BLK : (k + 1) * BLK, at : at + BLK] * col_ref[k]
        return turned(moments[k] * scales[k])

    last = nb + width // BLK

    def lanes_of(tiles):
        return slice(tiles[0] * BLK, (tiles[-1] + 1) * BLK)

    def updated(k, tiles):
        value = base(k, tiles[0])
        if len(tiles) > 1:
            value = jnp.concatenate([base(k, j) for j in tiles], axis=1)
        if k:
            rows, done = slice(k * BLK, (k + 1) * BLK), slice(0, k * BLK)
            value = value - dot3(
                [ref[rows, done] for ref in left], [ref[done, lanes_of(tiles)] for ref in right]
            )
        return value

    def prepare(k, tiles):
        panel_ref[k % 2, :, lanes_of(tiles)] = updated(k, tiles)

    z_tile = [None]

    def finish(k, tiles, inverse):
        rows, lanes = slice(k * BLK, (k + 1) * BLK), lanes_of(tiles)
        high, low = split2(panel_ref[k % 2, :, lanes])
        value = dot(inverse, jnp.concatenate([high, low, high], axis=0))
        if k + 1 < nb and tiles[0] > k:
            high, low = split2(value)
            right[0][rows, lanes] = high
            right[1][rows, lanes] = low
        for at, j in enumerate(tiles):
            one = value[:, at * BLK : (at + 1) * BLK]
            if j < nb:
                kept = one * root_ref[j : j + 1, :]
                if j == k:
                    kept = jnp.where(col_id >= row_id, kept, 0.0)
                else:
                    high, low = split2(one.T)
                    left[0][j * BLK : (j + 1) * BLK, rows] = high
                    left[1][j * BLK : (j + 1) * BLK, rows] = low
                full_ref[rows, j * BLK : (j + 1) * BLK] = kept
            elif j < last:
                at_x = (j - nb) * BLK
                part_x = jnp.sum(one * z_tile[0], axis=0, keepdims=True)
                if k:
                    part_x = part_x + x_ref[:, at_x : at_x + BLK]
                x_ref[:, at_x : at_x + BLK] = part_x
            else:
                z_tile[0] = one
                z_all[:, rows] = one.T[0:1, :]

    def groups(first_tile):
        found = [[last]]
        at = first_tile
        while at < last:
            size = 1 if at % 2 or at + 1 >= last or (at < nb <= at + 1) else 2
            found.append(list(range(at, at + size)))
            at += size
        return found

    queue = []
    for k in range(nb):
        d_ref[...] = updated(k, [k])
        panel_ref[k % 2, :, k * BLK : (k + 1) * BLK] = d_ref[...]
        queue += [functools.partial(prepare, k, tiles) for tiles in groups(k + 1)]
        factor_block(d_ref, inv_ref, cast_ref, times_ref, strip_ref, row_ref, queue)
        inv_high, inv_low = split2(inv_ref[...])
        inverse = jnp.concatenate([inv_high, inv_high, inv_low], axis=1)
        if k + 1 < nb:
            finish(k, [k + 1], inverse)
        queue += [functools.partial(finish, k, tiles, inverse) for tiles in groups(min(k + 2, nb))]
        queue.append(functools.partial(finish, k, [k], inverse))
    while queue:
        queue.pop(0)()

    rows = pl.ds(pl.multiple_of(me * out_rows, 8), out_rows)
    lanes = pl.ds(pl.multiple_of(core * width, BLK), width)
    r_ref[...] = full_ref[rows, lanes]
    z_ref[...] = z_all[:, lanes]


def per_device(
    whitening,
    sensor_states,
    sensor_coefficients,
    sensor_readings,
    conduit_endpoints,
    conductance,
    balance_right_side,
    prior_root_factor,
    prior_information,
    transition,
):
    n = prior_root_factor.shape[1]
    rows, cols = lax.axis_size("rows"), lax.axis_size("cols")
    plan = Plan(n, rows, cols)
    radix = plan.radix
    params = pltpu.CompilerParams(vmem_limit_bytes=VMEM_LIMIT)
    block_rows, bal_rows = whitening.shape[0], conductance.shape[0]
    depth = block_rows + bal_rows + BLK
    anywhere = pl.BlockSpec(memory_space=pl.ANY)
    hbm = pl.BlockSpec(memory_space=pltpu.HBM)
    vmem = pl.BlockSpec(memory_space=pltpu.VMEM)

    def typed(*shape):
        return jax.ShapeDtypeStruct(shape, F32)

    inputs = (
        whitening,
        sensor_states.T,
        sensor_coefficients.T,
        sensor_readings.reshape(-1, BLK),
        conduit_endpoints.T,
        conductance[None, :],
        balance_right_side[None, :],
        prior_root_factor,
        prior_information[None, :],
    )
    mine = pl.pallas_call(
        functools.partial(assemble_kernel, plan),
        out_shape=typed(rows * plan.piece, BLK),
        in_specs=[hbm] * len(inputs),
        out_specs=vmem,
        scratch_shapes=[pltpu.VMEM(x.shape, x.dtype) for x in inputs]
        + [
            pltpu.VMEM((n + 16, block_rows), BF16),
            pltpu.VMEM((n + 16, block_rows), BF16),
            pltpu.VMEM((n + 16, depth), BF16),
            pltpu.VMEM((n + 16, depth), BF16),
            pltpu.VMEM((BLK, n), F32),
            pltpu.VMEM((plan.total, BLK), F32),
            pltpu.SemaphoreType.DMA((len(inputs),)),
        ],
        compiler_params=pltpu.CompilerParams(vmem_limit_bytes=ASSEMBLE_VMEM),
        name="assemble",
    )(*inputs)

    spread = lax.all_to_all(
        mine.reshape(rows, plan.piece, BLK), "rows", split_axis=0, concat_axis=0
    )
    block = jnp.sum(spread, axis=0)

    def exchange(stage, rel, block):
        flip = rel * plan.stride[stage]
        return lax.ppermute(block, "rows", [(i, i ^ flip) for i in range(rows)])

    for stage in reversed(range(len(radix))):
        got = [block] + [exchange(stage, d, block) for d in range(1, radix[stage])]
        if stage:
            block = jnp.concatenate(got, axis=0)
    swap = [(i, i ^ 1) for i in range(cols)]
    both = got + [lax.ppermute(block, "cols", swap) for block in got]

    width = n // cols
    out_rows = n // rows
    wide = n + width + BLK
    r_post, z_post, x_next = pl.pallas_call(
        functools.partial(factor_kernel, plan, out_rows, width),
        out_shape=[typed(out_rows, width), typed(1, width), typed(1, width)],
        in_specs=[anywhere] * (len(both) + 1),
        out_specs=[vmem] * 3,
        scratch_shapes=[
            pltpu.VMEM((plan.total, BLK), F32),
            pltpu.VMEM((BLK, BLK), F32),
            pltpu.VMEM((BLK, BLK), F32),
            pltpu.VMEM((MIC * GRP, BLK), F32),
            pltpu.VMEM((MIC * MIC, BLK), F32),
            pltpu.VMEM((MIC, BLK), F32),
            pltpu.VMEM((MIC, BLK), F32),
            pltpu.VMEM((2, BLK, wide), F32),
            pltpu.VMEM((n, n), F32),
            pltpu.VMEM((n, width), F32),
            pltpu.VMEM((plan.blocks, BLK, BLK), F32),
            pltpu.VMEM((plan.blocks, BLK), F32),
            pltpu.VMEM((n, n), BF16),
            pltpu.VMEM((n, n), BF16),
            pltpu.VMEM((n, wide), BF16),
            pltpu.VMEM((n, wide), BF16),
            pltpu.VMEM((1, n), F32),
            pltpu.SemaphoreType.DMA((rows * cols,)),
            pltpu.SemaphoreType.DMA,
        ],
        compiler_params=params,
        name="factor",
    )(*both, transition.T)
    return (r_post, z_post[0], x_next[0])


def solution(mesh):
    in_specs = (
        P("rows", None),
        P("rows", None),
        P("rows", None),
        P("rows"),
        P("rows", None),
        P("rows"),
        P("rows"),
        P("rows", None),
        P("rows"),
        P("cols", None),
    )
    out_specs = (P("rows", "cols"), P("cols"), P("cols"))
    return jax.shard_map(
        per_device, mesh=mesh, in_specs=in_specs, out_specs=out_specs, check_vma=False
    )
```

```python
import functools

import jax
import jax.numpy as jnp
from jax import lax
from jax.experimental import pallas as pl
from jax.experimental.pallas import tpu as pltpu
from jax.sharding import PartitionSpec as P

BLK = 128
MIC = 32
GRP = 8
F32 = jnp.float32
BF16 = jnp.bfloat16
VMEM_LIMIT = 48 * 1024 * 1024
WHOLE_VMEM = 63 * 1024 * 1024


def split2(value):
    high = value.astype(BF16)
    low = (value - high.astype(F32)).astype(BF16)
    return high, low


def dot(left, right, left_dim=1, right_dim=0):
    return lax.dot_general(
        left, right, (((left_dim,), (right_dim,)), ((), ())), preferred_element_type=F32
    )


def dot3(left, right, left_dim=1, right_dim=0):
    total = dot(left[0], right[1], left_dim, right_dim) + dot(left[1], right[0], left_dim, right_dim)
    return total + dot(left[0], right[0], left_dim, right_dim)


def radices(count):
    found = []
    while count > 1:
        found.append(4 if count % 4 == 0 else 2)
        count //= found[-1]
    return tuple(found)


class Plan:
    def __init__(self, state_total, rows, cols):
        self.state_total = state_total
        self.blocks = nb = state_total // BLK
        self.rows, self.cols = rows, cols
        self.radix = radices(rows)
        self.stride = []
        step = 1
        for f in self.radix:
            self.stride.append(step)
            step *= f
        self.tiles = nb * (nb + 1) // 2
        unit = 8 * rows * cols
        self.total = -(-self.tiles * BLK // unit) * unit
        self.piece = self.total // (rows * cols)
        self.moment_rows = state_total // 64

    def digit(self, index, stage):
        return lax.rem(index // self.stride[stage], self.radix[stage])

    def span(self, stage):
        size = self.piece
        for f in self.radix[stage + 1 :]:
            size *= f
        return size

    def place(self, index, core):
        found = core
        for stride, f in zip(self.stride, self.radix):
            found = found * f + index // stride % f
        return found

    def tile(self, i, j):
        return (sum(self.blocks - k for k in range(i)) + j - i) * BLK


def assemble_kernel(plan, *refs):
    first = plan.radix[0]
    ins, outs, scratch = refs[:9], refs[9 : 9 + first], refs[9 + first :]
    here, (sens_hi, sens_lo, at_hi, at_lo, prior_pad, packed, sems) = scratch[:9], scratch[9:]
    copies = [pltpu.make_async_copy(a, b, sems.at[i]) for i, (a, b) in enumerate(zip(ins, here))]
    for copy in copies:
        copy.start()
    (
        white_ref,
        states_ref,
        coeffs_ref,
        readings_ref,
        ends_ref,
        conductance_ref,
        balance_rhs_ref,
        prior_ref,
        prior_info_ref,
    ) = here
    n = plan.state_total
    block_rows = white_ref.shape[0]
    bal_rows = conductance_ref.shape[1]
    prior_rows = prior_ref.shape[0]
    head = 16
    step = 64

    def put(high_ref, low_ref, row, col, value):
        high, low = split2(value)
        high_ref[row : row + value.shape[0], col : col + value.shape[1]] = high
        low_ref[row : row + value.shape[0], col : col + value.shape[1]] = low

    def head_rows(row):
        top = lax.broadcasted_iota(jnp.int32, (head, row.shape[1]), 0) == 0
        return jnp.where(top, jnp.broadcast_to(row, (head, row.shape[1])), 0.0)

    prior_pad[...] = jnp.zeros_like(prior_pad)
    if plan.tiles * BLK < plan.total:
        packed[plan.tiles * BLK :, :] = jnp.zeros((plan.total - plan.tiles * BLK, BLK), F32)
    for copy in copies:
        copy.wait()

    readings = jnp.concatenate(
        [readings_ref[k : k + 1, :] for k in range(readings_ref.shape[0])], axis=1
    )
    put(sens_hi, sens_lo, 0, 0, head_rows(readings))
    for at in range(0, n, step):
        ids = lax.broadcasted_iota(jnp.int32, (step, block_rows), 0) + at
        summed = jnp.zeros((step, block_rows), F32)
        for k in range(states_ref.shape[0]):
            summed = summed + jnp.where(ids == states_ref[k : k + 1, :], coeffs_ref[k : k + 1, :], 0.0)
        put(sens_hi, sens_lo, head + at, 0, summed)
    white = split2(white_ref[...])
    whitened = dot3((sens_hi[...], sens_lo[...]), white, 1, 1)
    for at in range(0, n + head, step):
        size = min(step, n + head - at)
        put(at_hi, at_lo, at, 0, whitened[at : at + size, :])

    conductance = conductance_ref[...]
    put(at_hi, at_lo, 0, block_rows, head_rows(conductance * balance_rhs_ref[...]))
    for at in range(0, n, step):
        ids = lax.broadcasted_iota(jnp.int32, (step, bal_rows), 0) + at
        value = jnp.where(ids == ends_ref[0:1, :], conductance, 0.0)
        value = value + jnp.where(ids == ends_ref[1:2, :], -conductance, 0.0)
        put(at_hi, at_lo, head + at, block_rows, value)

    prior_col = block_rows + bal_rows
    prior_pad[0:prior_rows, :] = prior_ref[...]
    info = jnp.concatenate([prior_info_ref[...], jnp.zeros((1, BLK - prior_rows), F32)], axis=1)
    put(at_hi, at_lo, 0, prior_col, head_rows(info))
    for at in range(0, n, BLK):
        put(at_hi, at_lo, head + at, prior_col, prior_pad[:, at : at + BLK].T)

    wide = 2 * BLK
    moments = []
    for at in range(0, n, wide):
        stop = head + at + wide
        out = dot3(
            (at_hi[0:stop, :], at_lo[0:stop, :]),
            (at_hi[head + at : stop, :], at_lo[head + at : stop, :]),
            1,
            1,
        )
        moments.append(out[0:1, :])
        for part in range(2):
            j = at // BLK + part
            for i in range(j + 1):
                row = plan.tile(i, j)
                packed[row : row + BLK, :] = out[
                    head + i * BLK : head + (i + 1) * BLK, part * BLK : (part + 1) * BLK
                ]
    for k in range(plan.moment_rows):
        row = BLK - plan.moment_rows + k
        source = moments[k * 64 // wide][:, k * 64 % wide : k * 64 % wide + 64]
        packed[row : row + 1, 0:64] = source

    me, core = lax.axis_index("rows"), lax.axis_index("cols")
    span = plan.span(0)
    for d in range(first):
        at = (core * first + (plan.digit(me, 0) ^ d)) * span
        outs[d][...] = packed[pl.ds(pl.multiple_of(at, 8), span), :]


def sum_kernel(plan, stage, *refs):
    before, after = plan.radix[stage - 1], plan.radix[stage]
    ins, outs = refs[:before], refs[before:]
    mine = plan.digit(lax.axis_index("rows"), stage)
    span = plan.span(stage)
    for d in range(after):
        rows = pl.ds(pl.multiple_of((mine ^ d) * span, 8), span)
        total = ins[0][rows, :]
        for other in ins[1:]:
            total = total + other[rows, :]
        outs[d][...] = total


def eliminate(s, rows):
    u = [[None] * GRP for _ in range(GRP)]
    pairs, done = [], []
    for p in range(0, GRP, 2):
        a, b, c = s[p][p], s[p + 1][p], s[p + 1][p + 1]
        det = a * c - b * b
        root_det = lax.rsqrt(det)
        root_a = lax.rsqrt(a)
        second = root_a * root_det
        inv = root_det * root_det
        u[p + 1][p] = b * root_a
        left = {}
        for i in range(p + 2, GRP):
            one, two = s[i][p], s[i][p + 1]
            cross = a * two - b * one
            left[i] = (c * one - b * two, cross)
            u[i][p] = one * root_a
            u[i][p + 1] = cross * second
        for c_at in range(p + 2, GRP):
            for i in range(c_at, GRP):
                fall = left[i][0] * s[c_at][p] + left[i][1] * s[c_at][p + 1]
                s[i][c_at] = s[i][c_at] - fall * inv
        pairs.append((a, b, root_a, second))
        done.append(rows[p] * root_a)
        done.append((a * rows[p + 1] - b * rows[p]) * second)
        for i in range(p + 2, GRP):
            rows[i] = rows[i] - (u[i][p] * done[p] + u[i][p + 1] * done[p + 1])
    return u, pairs, done


def factor_block(d_ref, inv_ref, cast_ref, times_ref, strip_ref, row_ref, queue):
    lane = lax.broadcasted_iota(jnp.int32, (MIC, BLK), 1)
    sub = lax.broadcasted_iota(jnp.int32, (MIC, BLK), 0)
    groups = MIC // GRP
    slots = groups * (BLK // MIC)
    share = -(-len(queue) // slots)

    def background():
        for _ in range(min(share, len(queue))):
            queue.pop(0)()

    for m in range(BLK // MIC):
        r0 = m * MIC
        strip = d_ref[r0 : r0 + MIC, :]
        inside = (lane >= r0) & (lane < r0 + MIC)
        ready = jnp.where(inside, jnp.where(lane == r0 + sub, 1.0, 0.0), strip)
        low, rest = [], []
        for g in range(groups):
            part = strip[g * GRP : (g + 1) * GRP, :]
            low.append(
                [
                    jnp.broadcast_to(part[:, r0 + c : r0 + c + 1], (GRP, BLK))
                    for c in range((g + 1) * GRP)
                ]
            )
            rest.append(ready[g * GRP : (g + 1) * GRP, :])
        for s in range(groups):
            base = s * GRP * GRP
            for c in range(GRP):
                cast_ref[base + GRP * c : base + GRP * (c + 1), :] = low[s][s * GRP + c]
            strip_ref[s * GRP : (s + 1) * GRP, :] = rest[s]
            splats = [
                [
                    cast_ref[base + GRP * c + i : base + GRP * c + i + 1, :] if i >= c else None
                    for c in range(GRP)
                ]
                for i in range(GRP)
            ]
            background()
            u, pairs, done = eliminate(
                splats, [strip_ref[s * GRP + i : s * GRP + i + 1, :] for i in range(GRP)]
            )
            for j in range(GRP):
                row_ref[s * GRP + j : s * GRP + j + 1, :] = done[j]
            for g in range(s + 1, groups):
                mine = low[g][s * GRP : (s + 1) * GRP]
                for p in range(0, GRP, 2):
                    a, b, root_a, second = pairs[p // 2]
                    one, two = mine[p], mine[p + 1]
                    mine[p] = one * root_a
                    mine[p + 1] = (a * two - b * one) * second
                    for c in range(p + 2, GRP):
                        mine[c] = mine[c] - (mine[p] * u[c][p] + mine[p + 1] * u[c][p + 1])
                times = (s * groups + g) * GRP * GRP
                for j in range(GRP):
                    times_ref[times + GRP * j : times + GRP * (j + 1), :] = mine[j]
                    rest[g] = rest[g] - mine[j] * done[j]
                for h in range(s + 1, g + 1):
                    other = (s * groups + h) * GRP * GRP
                    for c in range(GRP):
                        total = low[g][h * GRP + c]
                        for j in range(0, GRP, 2):
                            at = other + GRP * j + c
                            total = total - (
                                mine[j] * times_ref[at : at + 1, :]
                                + mine[j + 1] * times_ref[at + GRP : at + GRP + 1, :]
                            )
                        low[g][h * GRP + c] = total
        solved = row_ref[...]
        inv_ref[r0 : r0 + MIC, :] = jnp.where(lane < r0 + MIC, solved, 0.0)
        if r0 + MIC < BLK:
            high, low_part = split2(solved)
            fix = dot(
                jnp.concatenate([high, high, low_part], axis=0),
                jnp.concatenate([high, low_part, high], axis=0),
                0,
                0,
            )
            lanes = lax.broadcasted_iota(jnp.int32, (BLK - r0 - MIC, BLK), 1)
            keep = (lanes < r0) | (lanes >= r0 + MIC)
            left = jnp.where(keep, d_ref[r0 + MIC :, :], 0.0)
            d_ref[r0 + MIC :, :] = left - fix[r0 + MIC :, :]
    while queue:
        queue.pop(0)()


def factor_kernel(plan, out_rows, width, *refs):
    n, nb = plan.state_total, plan.blocks
    gathered, trans_hbm, r_ref, z_ref, x_ref, *scratch = refs
    (
        packed,
        d_ref,
        inv_ref,
        cast_ref,
        times_ref,
        strip_ref,
        row_ref,
        panel_ref,
        full_ref,
        trans_ref,
        col_ref,
        root_ref,
        *state,
        sems,
        trans_sem,
    ) = scratch
    left, right, z_all = state[:2], state[2:4], state[4]
    me, core = lax.axis_index("rows"), lax.axis_index("cols")

    copies = []
    for index in range(plan.rows):
        for e in range(plan.cols):
            source = (index * plan.cols + e) * plan.piece
            target = plan.place(index, e) * plan.piece
            copies.append(
                pltpu.make_async_copy(
                    gathered.at[pl.ds(source, plan.piece), :],
                    packed.at[pl.ds(target, plan.piece), :],
                    sems.at[len(copies)],
                )
            )
    trans_copy = pltpu.make_async_copy(trans_hbm, trans_ref, trans_sem)
    for copy in copies:
        copy.start()
    trans_copy.start()
    full_ref[...] = jnp.zeros_like(full_ref)
    for copy in copies:
        copy.wait()

    row_id = lax.broadcasted_iota(jnp.int32, (BLK, BLK), 0)
    col_id = lax.broadcasted_iota(jnp.int32, (BLK, BLK), 1)

    def turned(row):
        return jnp.broadcast_to(row, (BLK, BLK)).T

    tile = packed[0:BLK, :]
    hidden = (row_id >= BLK - plan.moment_rows) & (col_id < 64)
    moments = []
    for k in range(nb):
        at = BLK - plan.moment_rows + 2 * k
        moments.append(jnp.concatenate([tile[at : at + 1, 0:64], tile[at + 1 : at + 2, 0:64]], axis=1))
    packed[0:BLK, :] = jnp.where(hidden, tile.T, tile)

    scales = []
    for k in range(nb):
        row = plan.tile(k, k)
        diagonal = jnp.sum(
            jnp.where(row_id == col_id, packed[row : row + BLK, :], 0.0), axis=0, keepdims=True
        )
        scales.append(lax.rsqrt(diagonal))
        root_ref[k : k + 1, :] = diagonal * scales[k]
        col_ref[k] = turned(scales[k])
    trans_copy.wait()

    def base(k, j):
        if j < nb:
            row = plan.tile(k, j)
            return packed[row : row + BLK, :] * col_ref[k] * scales[j]
        if j < nb + width // BLK:
            at = (j - nb) * BLK
            return trans_ref[at : at + BLK, k * BLK : (k + 1) * BLK].T * col_ref[k]
        return turned(moments[k] * scales[k])

    last = nb + width // BLK

    def lanes_of(tiles):
        return slice(tiles[0] * BLK, (tiles[-1] + 1) * BLK)

    def updated(k, tiles):
        value = base(k, tiles[0])
        if len(tiles) > 1:
            value = jnp.concatenate([base(k, j) for j in tiles], axis=1)
        if k:
            rows, done = slice(k * BLK, (k + 1) * BLK), slice(0, k * BLK)
            value = value - dot3(
                [ref[rows, done] for ref in left], [ref[done, lanes_of(tiles)] for ref in right]
            )
        return value

    def prepare(k, tiles):
        panel_ref[k % 2, :, lanes_of(tiles)] = updated(k, tiles)

    z_tile = [None]

    def finish(k, tiles, inverse):
        rows, lanes = slice(k * BLK, (k + 1) * BLK), lanes_of(tiles)
        high, low = split2(panel_ref[k % 2, :, lanes])
        value = dot(inverse, jnp.concatenate([high, low, high], axis=0))
        if k + 1 < nb and tiles[0] > k:
            high, low = split2(value)
            right[0][rows, lanes] = high
            right[1][rows, lanes] = low
        for at, j in enumerate(tiles):
            one = value[:, at * BLK : (at + 1) * BLK]
            if j < nb:
                kept = one * root_ref[j : j + 1, :]
                if j == k:
                    kept = jnp.where(col_id >= row_id, kept, 0.0)
                else:
                    high, low = split2(one.T)
                    left[0][j * BLK : (j + 1) * BLK, rows] = high
                    left[1][j * BLK : (j + 1) * BLK, rows] = low
                full_ref[rows, j * BLK : (j + 1) * BLK] = kept
            elif j < last:
                at_x = (j - nb) * BLK
                part_x = jnp.sum(one * z_tile[0], axis=0, keepdims=True)
                if k:
                    part_x = part_x + x_ref[:, at_x : at_x + BLK]
                x_ref[:, at_x : at_x + BLK] = part_x
            else:
                z_tile[0] = one
                z_all[:, rows] = one.T[0:1, :]

    def groups(first_tile):
        found = [[last]]
        at = first_tile
        while at < last:
            size = 1 if at % 2 or at + 1 >= last or (at < nb <= at + 1) else 2
            found.append(list(range(at, at + size)))
            at += size
        return found

    queue = []
    for k in range(nb):
        d_ref[...] = updated(k, [k])
        panel_ref[k % 2, :, k * BLK : (k + 1) * BLK] = d_ref[...]
        queue += [functools.partial(prepare, k, tiles) for tiles in groups(k + 1)]
        factor_block(d_ref, inv_ref, cast_ref, times_ref, strip_ref, row_ref, queue)
        inv_high, inv_low = split2(inv_ref[...])
        inverse = jnp.concatenate([inv_high, inv_high, inv_low], axis=1)
        if k + 1 < nb:
            finish(k, [k + 1], inverse)
        queue += [functools.partial(finish, k, tiles, inverse) for tiles in groups(min(k + 2, nb))]
        queue.append(functools.partial(finish, k, [k], inverse))
    while queue:
        queue.pop(0)()

    rows = pl.ds(pl.multiple_of(me * out_rows, 8), out_rows)
    lanes = pl.ds(pl.multiple_of(core * width, BLK), width)
    r_ref[...] = full_ref[rows, lanes]
    z_ref[...] = z_all[:, lanes]


def per_device(
    whitening,
    sensor_states,
    sensor_coefficients,
    sensor_readings,
    conduit_endpoints,
    conductance,
    balance_right_side,
    prior_root_factor,
    prior_information,
    transition,
):
    n = prior_root_factor.shape[1]
    rows, cols = lax.axis_size("rows"), lax.axis_size("cols")
    plan = Plan(n, rows, cols)
    radix = plan.radix
    params = pltpu.CompilerParams(vmem_limit_bytes=VMEM_LIMIT)
    block_rows, bal_rows = whitening.shape[0], conductance.shape[0]
    depth = block_rows + bal_rows + BLK
    anywhere = pl.BlockSpec(memory_space=pl.ANY)
    hbm = pl.BlockSpec(memory_space=pltpu.HBM)
    vmem = pl.BlockSpec(memory_space=pltpu.VMEM)

    def typed(*shape):
        return jax.ShapeDtypeStruct(shape, F32)

    inputs = (
        whitening,
        sensor_states.T,
        sensor_coefficients.T,
        sensor_readings.reshape(-1, BLK),
        conduit_endpoints.T,
        conductance[None, :],
        balance_right_side[None, :],
        prior_root_factor,
        prior_information[None, :],
    )
    parts = pl.pallas_call(
        functools.partial(assemble_kernel, plan),
        out_shape=[typed(plan.span(0), BLK)] * radix[0],
        in_specs=[hbm] * len(inputs),
        out_specs=[vmem] * radix[0],
        scratch_shapes=[pltpu.VMEM(x.shape, x.dtype) for x in inputs]
        + [
            pltpu.VMEM((n + 16, block_rows), BF16),
            pltpu.VMEM((n + 16, block_rows), BF16),
            pltpu.VMEM((n + 16, depth), BF16),
            pltpu.VMEM((n + 16, depth), BF16),
            pltpu.VMEM((BLK, n), F32),
            pltpu.VMEM((plan.total, BLK), F32),
            pltpu.SemaphoreType.DMA((len(inputs),)),
        ],
        compiler_params=pltpu.CompilerParams(vmem_limit_bytes=WHOLE_VMEM),
        name="assemble",
    )(*inputs)

    def exchange(stage, rel, block):
        flip = rel * plan.stride[stage]
        return lax.ppermute(block, "rows", [(i, i ^ flip) for i in range(rows)])

    for stage in range(len(radix)):
        got = [parts[0]] + [exchange(stage, d, parts[d]) for d in range(1, radix[stage])]
        if stage + 1 < len(radix):
            parts = pl.pallas_call(
                functools.partial(sum_kernel, plan, stage + 1),
                out_shape=[typed(plan.span(stage + 1), BLK)] * radix[stage + 1],
                compiler_params=params,
                name="partial_sums",
            )(*got)
    block = functools.reduce(jnp.add, got)
    gathered = lax.all_gather(block, ("rows", "cols"), axis=0, tiled=True)

    width = n // cols
    out_rows = n // rows
    wide = n + width + BLK
    r_post, z_post, x_next = pl.pallas_call(
        functools.partial(factor_kernel, plan, out_rows, width),
        out_shape=[typed(out_rows, width), typed(1, width), typed(1, width)],
        in_specs=[anywhere] * 2,
        out_specs=[vmem] * 3,
        scratch_shapes=[
            pltpu.VMEM((plan.total, BLK), F32),
            pltpu.VMEM((BLK, BLK), F32),
            pltpu.VMEM((BLK, BLK), F32),
            pltpu.VMEM((MIC * GRP, BLK), F32),
            pltpu.VMEM((MIC * MIC, BLK), F32),
            pltpu.VMEM((MIC, BLK), F32),
            pltpu.VMEM((MIC, BLK), F32),
            pltpu.VMEM((2, BLK, wide), F32),
            pltpu.VMEM((n, n), F32),
            pltpu.VMEM((width, n), F32),
            pltpu.VMEM((plan.blocks, BLK, BLK), F32),
            pltpu.VMEM((plan.blocks, BLK), F32),
            pltpu.VMEM((n, n), BF16),
            pltpu.VMEM((n, n), BF16),
            pltpu.VMEM((n, wide), BF16),
            pltpu.VMEM((n, wide), BF16),
            pltpu.VMEM((1, n), F32),
            pltpu.SemaphoreType.DMA((rows * cols,)),
            pltpu.SemaphoreType.DMA,
        ],
        compiler_params=pltpu.CompilerParams(vmem_limit_bytes=WHOLE_VMEM),
        name="factor",
    )(gathered, transition)
    return (r_post, z_post[0], x_next[0])


def solution(mesh):
    in_specs = (
        P("rows", None),
        P("rows", None),
        P("rows", None),
        P("rows"),
        P("rows", None),
        P("rows"),
        P("rows"),
        P("rows", None),
        P("rows"),
        P("cols", None),
    )
    out_specs = (P("rows", "cols"), P("cols"), P("cols"))
    return jax.shard_map(
        per_device, mesh=mesh, in_specs=in_specs, out_specs=out_specs, check_vma=False
    )
```

```python
import functools

import jax
import jax.numpy as jnp
from jax import lax
from jax.experimental import pallas as pl
from jax.experimental.pallas import tpu as pltpu
from jax.sharding import PartitionSpec as P

BLK = 128
MIC = 32
GRP = 8
F32 = jnp.float32
BF16 = jnp.bfloat16
VMEM_LIMIT = 48 * 1024 * 1024
WHOLE_VMEM = 63 * 1024 * 1024


def split2(value):
    high = value.astype(BF16)
    low = (value - high.astype(F32)).astype(BF16)
    return high, low


def dot(left, right, left_dim=1, right_dim=0):
    return lax.dot_general(
        left, right, (((left_dim,), (right_dim,)), ((), ())), preferred_element_type=F32
    )


def dot3(left, right, left_dim=1, right_dim=0):
    total = dot(left[0], right[1], left_dim, right_dim) + dot(left[1], right[0], left_dim, right_dim)
    return total + dot(left[0], right[0], left_dim, right_dim)


def radices(count):
    found = []
    while count > 1:
        found.append(4 if count % 4 == 0 else 2)
        count //= found[-1]
    return tuple(found)


class Plan:
    def __init__(self, state_total, rows, cols):
        self.state_total = state_total
        self.blocks = nb = state_total // BLK
        self.rows, self.cols = rows, cols
        self.radix = radices(rows)
        self.stride = []
        step = 1
        for f in self.radix:
            self.stride.append(step)
            step *= f
        stages = list(range(len(self.radix)))
        self.orders = (stages, stages[::-1])
        tiles = [(i, j) for i in range(nb) for j in range(i, nb)]
        share = -(-len(tiles) // cols)
        piece = -(-share * BLK // (8 * rows)) * 8
        small = max(8, piece // 24 * 8)
        self.pieces = (piece - small, small)
        self.half = rows * piece
        self.local = {}
        for index, tile in enumerate(tiles):
            self.local[tile] = (index // share, index % share * BLK)
        self.moment_rows = state_total // 64

    def tile(self, i, j):
        core, row = self.local[i, j]
        return core * self.half + row

    def digit(self, index, stage):
        return lax.rem(index // self.stride[stage], self.radix[stage])

    def base(self, flow):
        return self.rows * self.pieces[0] * flow

    def span(self, flow, step):
        size = self.pieces[flow]
        for stage in self.orders[flow][step + 1 :]:
            size *= self.radix[stage]
        return size

    def fan(self, flow, step):
        return self.radix[self.orders[flow][step]]


def assemble_kernel(plan, *refs):
    fans = [plan.fan(flow, 0) for flow in range(2)]
    ins, outs, scratch = refs[:9], refs[9 : 9 + sum(fans)], refs[9 + sum(fans) :]
    here, (sens_hi, sens_lo, at_hi, at_lo, prior_pad, packed, sems) = scratch[:9], scratch[9:]
    copies = [pltpu.make_async_copy(a, b, sems.at[i]) for i, (a, b) in enumerate(zip(ins, here))]
    for copy in copies:
        copy.start()
    (
        white_ref,
        states_ref,
        coeffs_ref,
        readings_ref,
        ends_ref,
        conductance_ref,
        balance_rhs_ref,
        prior_ref,
        prior_info_ref,
    ) = here
    n = plan.state_total
    block_rows = white_ref.shape[0]
    bal_rows = conductance_ref.shape[1]
    prior_rows = prior_ref.shape[0]
    head = 16
    step = 64

    def put(high_ref, low_ref, row, col, value):
        high, low = split2(value)
        high_ref[row : row + value.shape[0], col : col + value.shape[1]] = high
        low_ref[row : row + value.shape[0], col : col + value.shape[1]] = low

    def head_rows(row):
        top = lax.broadcasted_iota(jnp.int32, (head, row.shape[1]), 0) == 0
        return jnp.where(top, jnp.broadcast_to(row, (head, row.shape[1])), 0.0)

    prior_pad[...] = jnp.zeros_like(prior_pad)
    used = max(row for _, row in plan.local.values()) + BLK
    if used < plan.half:
        packed[used:, :] = jnp.zeros((plan.half - used, BLK), F32)
    for copy in copies:
        copy.wait()

    readings = jnp.concatenate(
        [readings_ref[k : k + 1, :] for k in range(readings_ref.shape[0])], axis=1
    )
    put(sens_hi, sens_lo, 0, 0, head_rows(readings))
    for at in range(0, n, step):
        ids = lax.broadcasted_iota(jnp.int32, (step, block_rows), 0) + at
        summed = jnp.zeros((step, block_rows), F32)
        for k in range(states_ref.shape[0]):
            summed = summed + jnp.where(ids == states_ref[k : k + 1, :], coeffs_ref[k : k + 1, :], 0.0)
        put(sens_hi, sens_lo, head + at, 0, summed)
    white = split2(white_ref[...])
    whitened = dot3((sens_hi[...], sens_lo[...]), white, 1, 1)
    for at in range(0, n + head, step):
        size = min(step, n + head - at)
        put(at_hi, at_lo, at, 0, whitened[at : at + size, :])

    conductance = conductance_ref[...]
    put(at_hi, at_lo, 0, block_rows, head_rows(conductance * balance_rhs_ref[...]))
    for at in range(0, n, step):
        ids = lax.broadcasted_iota(jnp.int32, (step, bal_rows), 0) + at
        value = jnp.where(ids == ends_ref[0:1, :], conductance, 0.0)
        value = value + jnp.where(ids == ends_ref[1:2, :], -conductance, 0.0)
        put(at_hi, at_lo, head + at, block_rows, value)

    prior_col = block_rows + bal_rows
    prior_pad[0:prior_rows, :] = prior_ref[...]
    info = jnp.concatenate([prior_info_ref[...], jnp.zeros((1, BLK - prior_rows), F32)], axis=1)
    put(at_hi, at_lo, 0, prior_col, head_rows(info))
    for at in range(0, n, BLK):
        put(at_hi, at_lo, head + at, prior_col, prior_pad[:, at : at + BLK].T)

    me, core = lax.axis_index("rows"), lax.axis_index("cols")

    def tiles_of(part):
        moments = []
        for at in range(0, plan.blocks, 2):
            wanted = [(i, j) for (i, j), (c, _) in plan.local.items() if c == part and j // 2 == at // 2]
            if not wanted:
                continue
            low, high = min(i for i, _ in wanted), max(i for i, _ in wanted) + 1
            top = head + low * BLK if low else 0
            rows = slice(top, head + high * BLK)
            cols = slice(head + at * BLK, head + (at + 2) * BLK)
            out = dot3((at_hi[rows, :], at_lo[rows, :]), (at_hi[cols, :], at_lo[cols, :]), 1, 1)
            if not low:
                moments += [out[0:1, k * 64 : k * 64 + 64] for k in range(2 * BLK // 64)]
            for i, j in wanted:
                row, col = plan.local[i, j][1], (j - at) * BLK
                where = head + i * BLK - top
                packed[row : row + BLK, :] = out[where : where + BLK, col : col + BLK]
        for k, value in enumerate(moments):
            row = plan.local[0, 0][1] + BLK - plan.moment_rows + k
            packed[row : row + 1, 0:64] = value

    for part in range(plan.cols):
        pl.when(core == part)(functools.partial(tiles_of, part))

    outs = list(outs)
    for flow in range(2):
        span, stage = plan.span(flow, 0), plan.orders[flow][0]
        for d in range(fans[flow]):
            at = plan.base(flow) + (plan.digit(me, stage) ^ d) * span
            outs.pop(0)[...] = packed[pl.ds(pl.multiple_of(at, 8), span), :]


def sum_kernel(plan, step, *refs):
    me = lax.axis_index("rows")
    refs = list(refs)
    ins = [[refs.pop(0) for _ in range(plan.fan(flow, step))] for flow in range(2)]
    last = step + 1 == len(plan.radix)
    for flow in range(2):
        count = 1 if last else plan.fan(flow, step + 1)
        span = plan.span(flow, step + 1)
        for d in range(count):
            at = 0 if last else (plan.digit(me, plan.orders[flow][step + 1]) ^ d) * span
            rows = pl.ds(pl.multiple_of(at, 8), span)
            total = ins[flow][0][rows, :]
            for other in ins[flow][1:]:
                total = total + other[rows, :]
            refs.pop(0)[...] = total


def eliminate(s, rows):
    u = [[None] * GRP for _ in range(GRP)]
    pairs, done = [], []
    for p in range(0, GRP, 2):
        a, b, c = s[p][p], s[p + 1][p], s[p + 1][p + 1]
        det = a * c - b * b
        root_det = lax.rsqrt(det)
        root_a = lax.rsqrt(a)
        second = root_a * root_det
        inv = root_det * root_det
        u[p + 1][p] = b * root_a
        left = {}
        for i in range(p + 2, GRP):
            one, two = s[i][p], s[i][p + 1]
            cross = a * two - b * one
            left[i] = (c * one - b * two, cross)
            u[i][p] = one * root_a
            u[i][p + 1] = cross * second
        for c_at in range(p + 2, GRP):
            for i in range(c_at, GRP):
                fall = left[i][0] * s[c_at][p] + left[i][1] * s[c_at][p + 1]
                s[i][c_at] = s[i][c_at] - fall * inv
        pairs.append((a, b, root_a, second))
        done.append(rows[p] * root_a)
        done.append((a * rows[p + 1] - b * rows[p]) * second)
        for i in range(p + 2, GRP):
            rows[i] = rows[i] - (u[i][p] * done[p] + u[i][p + 1] * done[p + 1])
    return u, pairs, done


def factor_block(d_ref, inv_ref, cast_ref, times_ref, strip_ref, row_ref, queue):
    lane = lax.broadcasted_iota(jnp.int32, (MIC, BLK), 1)
    sub = lax.broadcasted_iota(jnp.int32, (MIC, BLK), 0)
    groups = MIC // GRP
    slots = groups * (BLK // MIC)
    share = -(-len(queue) // slots)

    def background():
        for _ in range(min(share, len(queue))):
            queue.pop(0)()

    for m in range(BLK // MIC):
        r0 = m * MIC
        strip = d_ref[r0 : r0 + MIC, :]
        inside = (lane >= r0) & (lane < r0 + MIC)
        ready = jnp.where(inside, jnp.where(lane == r0 + sub, 1.0, 0.0), strip)
        low, rest = [], []
        for g in range(groups):
            part = strip[g * GRP : (g + 1) * GRP, :]
            low.append(
                [
                    jnp.broadcast_to(part[:, r0 + c : r0 + c + 1], (GRP, BLK))
                    for c in range((g + 1) * GRP)
                ]
            )
            rest.append(ready[g * GRP : (g + 1) * GRP, :])
        for s in range(groups):
            base = s * GRP * GRP
            for c in range(GRP):
                cast_ref[base + GRP * c : base + GRP * (c + 1), :] = low[s][s * GRP + c]
            strip_ref[s * GRP : (s + 1) * GRP, :] = rest[s]
            splats = [
                [
                    cast_ref[base + GRP * c + i : base + GRP * c + i + 1, :] if i >= c else None
                    for c in range(GRP)
                ]
                for i in range(GRP)
            ]
            background()
            u, pairs, done = eliminate(
                splats, [strip_ref[s * GRP + i : s * GRP + i + 1, :] for i in range(GRP)]
            )
            for j in range(GRP):
                row_ref[s * GRP + j : s * GRP + j + 1, :] = done[j]
            for g in range(s + 1, groups):
                mine = low[g][s * GRP : (s + 1) * GRP]
                for p in range(0, GRP, 2):
                    a, b, root_a, second = pairs[p // 2]
                    one, two = mine[p], mine[p + 1]
                    mine[p] = one * root_a
                    mine[p + 1] = (a * two - b * one) * second
                    for c in range(p + 2, GRP):
                        mine[c] = mine[c] - (mine[p] * u[c][p] + mine[p + 1] * u[c][p + 1])
                times = (s * groups + g) * GRP * GRP
                for j in range(GRP):
                    times_ref[times + GRP * j : times + GRP * (j + 1), :] = mine[j]
                    rest[g] = rest[g] - mine[j] * done[j]
                for h in range(s + 1, g + 1):
                    other = (s * groups + h) * GRP * GRP
                    for c in range(GRP):
                        total = low[g][h * GRP + c]
                        for j in range(0, GRP, 2):
                            at = other + GRP * j + c
                            total = total - (
                                mine[j] * times_ref[at : at + 1, :]
                                + mine[j + 1] * times_ref[at + GRP : at + GRP + 1, :]
                            )
                        low[g][h * GRP + c] = total
        solved = row_ref[...]
        inv_ref[r0 : r0 + MIC, :] = jnp.where(lane < r0 + MIC, solved, 0.0)
        if r0 + MIC < BLK:
            high, low_part = split2(solved)
            fix = dot(
                jnp.concatenate([high, high, low_part], axis=0),
                jnp.concatenate([high, low_part, high], axis=0),
                0,
                0,
            )
            lanes = lax.broadcasted_iota(jnp.int32, (BLK - r0 - MIC, BLK), 1)
            keep = (lanes < r0) | (lanes >= r0 + MIC)
            left = jnp.where(keep, d_ref[r0 + MIC :, :], 0.0)
            d_ref[r0 + MIC :, :] = left - fix[r0 + MIC :, :]
    while queue:
        queue.pop(0)()


def factor_kernel(plan, out_rows, width, *refs):
    n, nb = plan.state_total, plan.blocks
    slots = max(plan.fan(flow, 0) for flow in range(2))
    ins, (trans_hbm, r_ref, z_ref, x_ref, *scratch) = refs[: slots * plan.cols], refs[slots * plan.cols :]
    (
        packed,
        d_ref,
        inv_ref,
        cast_ref,
        times_ref,
        strip_ref,
        row_ref,
        panel_ref,
        full_ref,
        trans_ref,
        col_ref,
        root_ref,
        *state,
        sems,
        trans_sem,
    ) = scratch
    left, right, z_all = state[:2], state[2:4], state[4]
    me, core = lax.axis_index("rows"), lax.axis_index("cols")

    copies = []
    for e in range(plan.cols):
        offsets = [0] * slots
        for flow in range(2):
            piece, order = plan.pieces[flow], plan.orders[flow]
            inner = plan.span(flow, 0) // piece
            for d in range(plan.fan(flow, 0)):
                for f in range(inner):
                    place = plan.digit(me, order[0]) ^ d
                    rest, size = f, inner
                    for stage in order[1:]:
                        size //= plan.radix[stage]
                        place = place * plan.radix[stage] + (plan.digit(me, stage) ^ (rest // size))
                        rest %= size
                    target = (core ^ e) * plan.half + plan.base(flow) + place * piece
                    copies.append(
                        pltpu.make_async_copy(
                            ins[e * slots + d].at[pl.ds(offsets[d] + f * piece, piece), :],
                            packed.at[pl.ds(pl.multiple_of(target, 8), piece), :],
                            sems.at[len(copies)],
                        )
                    )
                offsets[d] += inner * piece
    trans_copy = pltpu.make_async_copy(trans_hbm, trans_ref, trans_sem)
    for copy in copies:
        copy.start()
    trans_copy.start()
    full_ref[...] = jnp.zeros_like(full_ref)
    for copy in copies:
        copy.wait()

    row_id = lax.broadcasted_iota(jnp.int32, (BLK, BLK), 0)
    col_id = lax.broadcasted_iota(jnp.int32, (BLK, BLK), 1)

    def turned(row):
        return jnp.broadcast_to(row, (BLK, BLK)).T

    corner = plan.tile(0, 0)
    tile = packed[corner : corner + BLK, :]
    hidden = (row_id >= BLK - plan.moment_rows) & (col_id < 64)
    moments = []
    for k in range(nb):
        at = BLK - plan.moment_rows + 2 * k
        moments.append(jnp.concatenate([tile[at : at + 1, 0:64], tile[at + 1 : at + 2, 0:64]], axis=1))
    packed[corner : corner + BLK, :] = jnp.where(hidden, tile.T, tile)

    scales = []
    for k in range(nb):
        row = plan.tile(k, k)
        diagonal = jnp.sum(
            jnp.where(row_id == col_id, packed[row : row + BLK, :], 0.0), axis=0, keepdims=True
        )
        scales.append(lax.rsqrt(diagonal))
        root_ref[k : k + 1, :] = diagonal * scales[k]
        col_ref[k] = turned(scales[k])
    trans_copy.wait()

    def base(k, j):
        if j < nb:
            row = plan.tile(k, j)
            return packed[row : row + BLK, :] * col_ref[k] * scales[j]
        if j < nb + width // BLK:
            at = (j - nb) * BLK
            return trans_ref[at : at + BLK, k * BLK : (k + 1) * BLK].T * col_ref[k]
        return turned(moments[k] * scales[k])

    last = nb + width // BLK

    def lanes_of(tiles):
        return slice(tiles[0] * BLK, (tiles[-1] + 1) * BLK)

    def updated(k, tiles):
        value = base(k, tiles[0])
        if len(tiles) > 1:
            value = jnp.concatenate([base(k, j) for j in tiles], axis=1)
        if k:
            rows, done = slice(k * BLK, (k + 1) * BLK), slice(0, k * BLK)
            value = value - dot3(
                [ref[rows, done] for ref in left], [ref[done, lanes_of(tiles)] for ref in right]
            )
        return value

    def prepare(k, tiles):
        panel_ref[k % 2, :, lanes_of(tiles)] = updated(k, tiles)

    z_tile = [None]

    def finish(k, tiles, inverse):
        rows, lanes = slice(k * BLK, (k + 1) * BLK), lanes_of(tiles)
        high, low = split2(panel_ref[k % 2, :, lanes])
        value = dot(inverse, jnp.concatenate([high, low, high], axis=0))
        if k + 1 < nb and tiles[0] > k:
            high, low = split2(value)
            right[0][rows, lanes] = high
            right[1][rows, lanes] = low
        for at, j in enumerate(tiles):
            one = value[:, at * BLK : (at + 1) * BLK]
            if j < nb:
                kept = one * root_ref[j : j + 1, :]
                if j == k:
                    kept = jnp.where(col_id >= row_id, kept, 0.0)
                else:
                    high, low = split2(one.T)
                    left[0][j * BLK : (j + 1) * BLK, rows] = high
                    left[1][j * BLK : (j + 1) * BLK, rows] = low
                full_ref[rows, j * BLK : (j + 1) * BLK] = kept
            elif j < last:
                at_x = (j - nb) * BLK
                part_x = jnp.sum(one * z_tile[0], axis=0, keepdims=True)
                if k:
                    part_x = part_x + x_ref[:, at_x : at_x + BLK]
                x_ref[:, at_x : at_x + BLK] = part_x
            else:
                z_tile[0] = one
                z_all[:, rows] = one.T[0:1, :]

    def groups(first_tile):
        found = [[last]]
        at = first_tile
        while at < last:
            size = 1 if at % 2 or at + 1 >= last or (at < nb <= at + 1) else 2
            found.append(list(range(at, at + size)))
            at += size
        return found

    queue = []
    for k in range(nb):
        d_ref[...] = updated(k, [k])
        panel_ref[k % 2, :, k * BLK : (k + 1) * BLK] = d_ref[...]
        queue += [functools.partial(prepare, k, tiles) for tiles in groups(k + 1)]
        factor_block(d_ref, inv_ref, cast_ref, times_ref, strip_ref, row_ref, queue)
        inv_high, inv_low = split2(inv_ref[...])
        inverse = jnp.concatenate([inv_high, inv_high, inv_low], axis=1)
        if k + 1 < nb:
            finish(k, [k + 1], inverse)
        queue += [functools.partial(finish, k, tiles, inverse) for tiles in groups(min(k + 2, nb))]
        queue.append(functools.partial(finish, k, [k], inverse))
    while queue:
        queue.pop(0)()

    rows = pl.ds(pl.multiple_of(me * out_rows, 8), out_rows)
    lanes = pl.ds(pl.multiple_of(core * width, BLK), width)
    r_ref[...] = full_ref[rows, lanes]
    z_ref[...] = z_all[:, lanes]


def per_device(
    whitening,
    sensor_states,
    sensor_coefficients,
    sensor_readings,
    conduit_endpoints,
    conductance,
    balance_right_side,
    prior_root_factor,
    prior_information,
    transition,
):
    n = prior_root_factor.shape[1]
    rows, cols = lax.axis_size("rows"), lax.axis_size("cols")
    plan = Plan(n, rows, cols)
    radix = plan.radix
    params = pltpu.CompilerParams(vmem_limit_bytes=VMEM_LIMIT)
    block_rows, bal_rows = whitening.shape[0], conductance.shape[0]
    depth = block_rows + bal_rows + BLK
    anywhere = pl.BlockSpec(memory_space=pl.ANY)
    hbm = pl.BlockSpec(memory_space=pltpu.HBM)
    vmem = pl.BlockSpec(memory_space=pltpu.VMEM)

    def typed(*shape):
        return jax.ShapeDtypeStruct(shape, F32)

    inputs = (
        whitening,
        sensor_states.T,
        sensor_coefficients.T,
        sensor_readings.reshape(-1, BLK),
        conduit_endpoints.T,
        conductance[None, :],
        balance_right_side[None, :],
        prior_root_factor,
        prior_information[None, :],
    )
    parts = pl.pallas_call(
        functools.partial(assemble_kernel, plan),
        out_shape=[typed(plan.span(f, 0), BLK) for f in range(2) for _ in range(plan.fan(f, 0))],
        in_specs=[hbm] * len(inputs),
        out_specs=[vmem] * sum(plan.fan(f, 0) for f in range(2)),
        scratch_shapes=[pltpu.VMEM(x.shape, x.dtype) for x in inputs]
        + [
            pltpu.VMEM((n + 16, block_rows), BF16),
            pltpu.VMEM((n + 16, block_rows), BF16),
            pltpu.VMEM((n + 16, depth), BF16),
            pltpu.VMEM((n + 16, depth), BF16),
            pltpu.VMEM((BLK, n), F32),
            pltpu.VMEM((plan.half, BLK), F32),
            pltpu.SemaphoreType.DMA((len(inputs),)),
        ],
        compiler_params=pltpu.CompilerParams(vmem_limit_bytes=WHOLE_VMEM),
        name="assemble",
    )(*inputs)

    def exchange(stage, rel, block):
        flip = rel * plan.stride[stage]
        return lax.ppermute(block, "rows", [(i, i ^ flip) for i in range(rows)])

    steps = len(radix)
    for step in range(steps):
        parts = list(parts)
        got = []
        for flow in range(2):
            fan, stage = plan.fan(flow, step), plan.orders[flow][step]
            mine = [parts.pop(0) for _ in range(fan)]
            got += mine[:1] + [exchange(stage, d, mine[d]) for d in range(1, fan)]
        last = step + 1 == steps
        shapes = [
            typed(plan.span(flow, step + 1), BLK)
            for flow in range(2)
            for _ in range(1 if last else plan.fan(flow, step + 1))
        ]
        parts = pl.pallas_call(
            functools.partial(sum_kernel, plan, step),
            out_shape=shapes,
            compiler_params=params,
            name="partial_sums",
        )(*got)
    blocks = list(parts)
    for step in reversed(range(steps)):
        got = []
        for flow in range(2):
            fan, stage = plan.fan(flow, step), plan.orders[flow][step]
            got.append([blocks[flow]] + [exchange(stage, d, blocks[flow]) for d in range(1, fan)])
        if step:
            blocks = [jnp.concatenate(found, axis=0) for found in got]
    swap = [(i, i ^ 1) for i in range(cols)]
    joined = [
        jnp.concatenate([found[d] for found in got if d < len(found)], axis=0)
        for d in range(max(len(found) for found in got))
    ]
    both = joined + [lax.ppermute(block, "cols", swap) for block in joined]

    width = n // cols
    out_rows = n // rows
    wide = n + width + BLK
    r_post, z_post, x_next = pl.pallas_call(
        functools.partial(factor_kernel, plan, out_rows, width),
        out_shape=[typed(out_rows, width), typed(1, width), typed(1, width)],
        in_specs=[anywhere] * (len(both) + 1),
        out_specs=[vmem] * 3,
        scratch_shapes=[
            pltpu.VMEM((cols * plan.half, BLK), F32),
            pltpu.VMEM((BLK, BLK), F32),
            pltpu.VMEM((BLK, BLK), F32),
            pltpu.VMEM((MIC * GRP, BLK), F32),
            pltpu.VMEM((MIC * MIC, BLK), F32),
            pltpu.VMEM((MIC, BLK), F32),
            pltpu.VMEM((MIC, BLK), F32),
            pltpu.VMEM((2, BLK, wide), F32),
            pltpu.VMEM((n, n), F32),
            pltpu.VMEM((width, n), F32),
            pltpu.VMEM((plan.blocks, BLK, BLK), F32),
            pltpu.VMEM((plan.blocks, BLK), F32),
            pltpu.VMEM((n, n), BF16),
            pltpu.VMEM((n, n), BF16),
            pltpu.VMEM((n, wide), BF16),
            pltpu.VMEM((n, wide), BF16),
            pltpu.VMEM((1, n), F32),
            pltpu.SemaphoreType.DMA((2 * rows * cols,)),
            pltpu.SemaphoreType.DMA,
        ],
        compiler_params=params,
        name="factor",
    )(*both, transition)
    return (r_post, z_post[0], x_next[0])


def solution(mesh):
    in_specs = (
        P("rows", None),
        P("rows", None),
        P("rows", None),
        P("rows"),
        P("rows", None),
        P("rows"),
        P("rows"),
        P("rows", None),
        P("rows"),
        P("cols", None),
    )
    out_specs = (P("rows", "cols"), P("cols"), P("cols"))
    return jax.shard_map(
        per_device, mesh=mesh, in_specs=in_specs, out_specs=out_specs, check_vma=False
    )
```

```python
import functools

import jax
import jax.numpy as jnp
from jax import lax
from jax.experimental import pallas as pl
from jax.experimental.pallas import tpu as pltpu
from jax.sharding import PartitionSpec as P

BLK = 128
MIC = 32
GRP = 8
F32 = jnp.float32
BF16 = jnp.bfloat16
VMEM_LIMIT = 48 * 1024 * 1024
WHOLE_VMEM = 63 * 1024 * 1024


def split2(value):
    high = value.astype(BF16)
    low = (value - high.astype(F32)).astype(BF16)
    return high, low


def dot(left, right, left_dim=1, right_dim=0):
    return lax.dot_general(
        left, right, (((left_dim,), (right_dim,)), ((), ())), preferred_element_type=F32
    )


def dot3(left, right, left_dim=1, right_dim=0):
    total = dot(left[0], right[1], left_dim, right_dim) + dot(left[1], right[0], left_dim, right_dim)
    return total + dot(left[0], right[0], left_dim, right_dim)


def radices(count):
    found = []
    while count > 1:
        found.append(4 if count % 4 == 0 else 2)
        count //= found[-1]
    return tuple(found)


class Plan:
    def __init__(self, state_total, rows, cols):
        self.state_total = state_total
        self.blocks = nb = state_total // BLK
        self.rows, self.cols = rows, cols
        self.radix = radices(rows)
        self.stride = []
        step = 1
        for f in self.radix:
            self.stride.append(step)
            step *= f
        stages = list(range(len(self.radix)))
        self.orders = (stages,)
        tiles = [(i, j) for i in range(nb) for j in range(i, nb)]
        share = -(-len(tiles) // cols)
        piece = -(-share * BLK // (8 * rows)) * 8
        self.pieces = (piece,)
        self.half = rows * piece
        self.local = {}
        for index, tile in enumerate(tiles):
            self.local[tile] = (index // share, index % share * BLK)
        self.moment_rows = state_total // 64

    def tile(self, i, j):
        core, row = self.local[i, j]
        return core * self.half + row

    def digit(self, index, stage):
        return lax.rem(index // self.stride[stage], self.radix[stage])

    def base(self, flow):
        return self.rows * self.pieces[0] * flow

    def span(self, flow, step):
        size = self.pieces[flow]
        for stage in self.orders[flow][step + 1 :]:
            size *= self.radix[stage]
        return size

    def fan(self, flow, step):
        return self.radix[self.orders[flow][step]]


def assemble_kernel(plan, *refs):
    fans = [plan.fan(flow, 0) for flow in range(len(plan.orders))]
    ins, outs, scratch = refs[:9], refs[9 : 9 + sum(fans)], refs[9 + sum(fans) :]
    here, (sens_hi, sens_lo, at_hi, at_lo, prior_pad, packed, sems) = scratch[:9], scratch[9:]
    copies = [pltpu.make_async_copy(a, b, sems.at[i]) for i, (a, b) in enumerate(zip(ins, here))]
    for copy in copies:
        copy.start()
    (
        white_ref,
        states_ref,
        coeffs_ref,
        readings_ref,
        ends_ref,
        conductance_ref,
        balance_rhs_ref,
        prior_ref,
        prior_info_ref,
    ) = here
    n = plan.state_total
    block_rows = white_ref.shape[0]
    bal_rows = conductance_ref.shape[1]
    prior_rows = prior_ref.shape[0]
    head = 16
    step = 64

    def put(high_ref, low_ref, row, col, value):
        high, low = split2(value)
        high_ref[row : row + value.shape[0], col : col + value.shape[1]] = high
        low_ref[row : row + value.shape[0], col : col + value.shape[1]] = low

    def head_rows(row):
        top = lax.broadcasted_iota(jnp.int32, (head, row.shape[1]), 0) == 0
        return jnp.where(top, jnp.broadcast_to(row, (head, row.shape[1])), 0.0)

    prior_pad[...] = jnp.zeros_like(prior_pad)
    used = max(row for _, row in plan.local.values()) + BLK
    if used < plan.half:
        packed[used:, :] = jnp.zeros((plan.half - used, BLK), F32)
    for copy in copies:
        copy.wait()

    readings = jnp.concatenate(
        [readings_ref[k : k + 1, :] for k in range(readings_ref.shape[0])], axis=1
    )
    put(sens_hi, sens_lo, 0, 0, head_rows(readings))
    for at in range(0, n, step):
        ids = lax.broadcasted_iota(jnp.int32, (step, block_rows), 0) + at
        summed = jnp.zeros((step, block_rows), F32)
        for k in range(states_ref.shape[0]):
            summed = summed + jnp.where(ids == states_ref[k : k + 1, :], coeffs_ref[k : k + 1, :], 0.0)
        put(sens_hi, sens_lo, head + at, 0, summed)
    white = split2(white_ref[...])
    whitened = dot3((sens_hi[...], sens_lo[...]), white, 1, 1)
    for at in range(0, n + head, step):
        size = min(step, n + head - at)
        put(at_hi, at_lo, at, 0, whitened[at : at + size, :])

    conductance = conductance_ref[...]
    put(at_hi, at_lo, 0, block_rows, head_rows(conductance * balance_rhs_ref[...]))
    for at in range(0, n, step):
        ids = lax.broadcasted_iota(jnp.int32, (step, bal_rows), 0) + at
        value = jnp.where(ids == ends_ref[0:1, :], conductance, 0.0)
        value = value + jnp.where(ids == ends_ref[1:2, :], -conductance, 0.0)
        put(at_hi, at_lo, head + at, block_rows, value)

    prior_col = block_rows + bal_rows
    prior_pad[0:prior_rows, :] = prior_ref[...]
    info = jnp.concatenate([prior_info_ref[...], jnp.zeros((1, BLK - prior_rows), F32)], axis=1)
    put(at_hi, at_lo, 0, prior_col, head_rows(info))
    for at in range(0, n, BLK):
        put(at_hi, at_lo, head + at, prior_col, prior_pad[:, at : at + BLK].T)

    me, core = lax.axis_index("rows"), lax.axis_index("cols")

    def tiles_of(part):
        moments = []
        for at in range(0, plan.blocks, 2):
            wanted = [(i, j) for (i, j), (c, _) in plan.local.items() if c == part and j // 2 == at // 2]
            if not wanted:
                continue
            low, high = min(i for i, _ in wanted), max(i for i, _ in wanted) + 1
            top = head + low * BLK if low else 0
            rows = slice(top, head + high * BLK)
            cols = slice(head + at * BLK, head + (at + 2) * BLK)
            out = dot3((at_hi[rows, :], at_lo[rows, :]), (at_hi[cols, :], at_lo[cols, :]), 1, 1)
            if not low:
                moments += [out[0:1, k * 64 : k * 64 + 64] for k in range(2 * BLK // 64)]
            for i, j in wanted:
                row, col = plan.local[i, j][1], (j - at) * BLK
                where = head + i * BLK - top
                packed[row : row + BLK, :] = out[where : where + BLK, col : col + BLK]
        for k, value in enumerate(moments):
            row = plan.local[0, 0][1] + BLK - plan.moment_rows + k
            packed[row : row + 1, 0:64] = value

    for part in range(plan.cols):
        pl.when(core == part)(functools.partial(tiles_of, part))

    outs = list(outs)
    for flow in range(len(plan.orders)):
        span, stage = plan.span(flow, 0), plan.orders[flow][0]
        for d in range(fans[flow]):
            at = plan.base(flow) + (plan.digit(me, stage) ^ d) * span
            outs.pop(0)[...] = packed[pl.ds(pl.multiple_of(at, 8), span), :]


def sum_kernel(plan, step, *refs):
    me = lax.axis_index("rows")
    refs = list(refs)
    ins = [[refs.pop(0) for _ in range(plan.fan(flow, step))] for flow in range(len(plan.orders))]
    last = step + 1 == len(plan.radix)
    for flow in range(len(plan.orders)):
        count = 1 if last else plan.fan(flow, step + 1)
        span = plan.span(flow, step + 1)
        for d in range(count):
            at = 0 if last else (plan.digit(me, plan.orders[flow][step + 1]) ^ d) * span
            rows = pl.ds(pl.multiple_of(at, 8), span)
            total = ins[flow][0][rows, :]
            for other in ins[flow][1:]:
                total = total + other[rows, :]
            refs.pop(0)[...] = total


def eliminate(s, rows):
    u = [[None] * GRP for _ in range(GRP)]
    pairs, done = [], []
    for p in range(0, GRP, 2):
        a, b, c = s[p][p], s[p + 1][p], s[p + 1][p + 1]
        det = a * c - b * b
        root_det = lax.rsqrt(det)
        root_a = lax.rsqrt(a)
        second = root_a * root_det
        inv = root_det * root_det
        u[p + 1][p] = b * root_a
        left = {}
        for i in range(p + 2, GRP):
            one, two = s[i][p], s[i][p + 1]
            cross = a * two - b * one
            left[i] = (c * one - b * two, cross)
            u[i][p] = one * root_a
            u[i][p + 1] = cross * second
        for c_at in range(p + 2, GRP):
            for i in range(c_at, GRP):
                fall = left[i][0] * s[c_at][p] + left[i][1] * s[c_at][p + 1]
                s[i][c_at] = s[i][c_at] - fall * inv
        pairs.append((a, b, root_a, second))
        done.append(rows[p] * root_a)
        done.append((a * rows[p + 1] - b * rows[p]) * second)
        for i in range(p + 2, GRP):
            rows[i] = rows[i] - (u[i][p] * done[p] + u[i][p + 1] * done[p + 1])
    return u, pairs, done


def factor_block(d_ref, inv_ref, cast_ref, times_ref, strip_ref, row_ref, queue):
    lane = lax.broadcasted_iota(jnp.int32, (MIC, BLK), 1)
    sub = lax.broadcasted_iota(jnp.int32, (MIC, BLK), 0)
    groups = MIC // GRP
    slots = groups * (BLK // MIC)
    share = -(-len(queue) // slots)

    def background():
        for _ in range(min(share, len(queue))):
            queue.pop(0)()

    for m in range(BLK // MIC):
        r0 = m * MIC
        strip = d_ref[r0 : r0 + MIC, :]
        inside = (lane >= r0) & (lane < r0 + MIC)
        ready = jnp.where(inside, jnp.where(lane == r0 + sub, 1.0, 0.0), strip)
        low, rest = [], []
        for g in range(groups):
            part = strip[g * GRP : (g + 1) * GRP, :]
            low.append(
                [
                    jnp.broadcast_to(part[:, r0 + c : r0 + c + 1], (GRP, BLK))
                    for c in range((g + 1) * GRP)
                ]
            )
            rest.append(ready[g * GRP : (g + 1) * GRP, :])
        for s in range(groups):
            base = s * GRP * GRP
            for c in range(GRP):
                cast_ref[base + GRP * c : base + GRP * (c + 1), :] = low[s][s * GRP + c]
            strip_ref[s * GRP : (s + 1) * GRP, :] = rest[s]
            splats = [
                [
                    cast_ref[base + GRP * c + i : base + GRP * c + i + 1, :] if i >= c else None
                    for c in range(GRP)
                ]
                for i in range(GRP)
            ]
            background()
            u, pairs, done = eliminate(
                splats, [strip_ref[s * GRP + i : s * GRP + i + 1, :] for i in range(GRP)]
            )
            for j in range(GRP):
                row_ref[s * GRP + j : s * GRP + j + 1, :] = done[j]
            for g in range(s + 1, groups):
                mine = low[g][s * GRP : (s + 1) * GRP]
                for p in range(0, GRP, 2):
                    a, b, root_a, second = pairs[p // 2]
                    one, two = mine[p], mine[p + 1]
                    mine[p] = one * root_a
                    mine[p + 1] = (a * two - b * one) * second
                    for c in range(p + 2, GRP):
                        mine[c] = mine[c] - (mine[p] * u[c][p] + mine[p + 1] * u[c][p + 1])
                times = (s * groups + g) * GRP * GRP
                for j in range(GRP):
                    times_ref[times + GRP * j : times + GRP * (j + 1), :] = mine[j]
                    rest[g] = rest[g] - mine[j] * done[j]
                for h in range(s + 1, g + 1):
                    other = (s * groups + h) * GRP * GRP
                    for c in range(GRP):
                        total = low[g][h * GRP + c]
                        for j in range(0, GRP, 2):
                            at = other + GRP * j + c
                            total = total - (
                                mine[j] * times_ref[at : at + 1, :]
                                + mine[j + 1] * times_ref[at + GRP : at + GRP + 1, :]
                            )
                        low[g][h * GRP + c] = total
        solved = row_ref[...]
        inv_ref[r0 : r0 + MIC, :] = jnp.where(lane < r0 + MIC, solved, 0.0)
        if r0 + MIC < BLK:
            fix = dot3(split2(solved.T[r0 + MIC :, :]), split2(solved))
            lanes = lax.broadcasted_iota(jnp.int32, (BLK - r0 - MIC, BLK), 1)
            keep = (lanes < r0) | (lanes >= r0 + MIC)
            left = jnp.where(keep, d_ref[r0 + MIC :, :], 0.0)
            d_ref[r0 + MIC :, :] = left - fix
    while queue:
        queue.pop(0)()


def factor_kernel(plan, out_rows, width, *refs):
    n, nb = plan.state_total, plan.blocks
    slots = max(plan.fan(flow, 0) for flow in range(len(plan.orders)))
    ins, (trans_hbm, r_ref, z_ref, x_ref, *scratch) = refs[: slots * plan.cols], refs[slots * plan.cols :]
    (
        packed,
        d_ref,
        inv_ref,
        cast_ref,
        times_ref,
        strip_ref,
        row_ref,
        panel_ref,
        turn_ref,
        next_ref,
        full_ref,
        trans_ref,
        col_ref,
        root_ref,
        *state,
        sems,
        trans_sem,
    ) = scratch
    left, right, z_all = state[:2], state[2:4], state[4]
    me, core = lax.axis_index("rows"), lax.axis_index("cols")

    copies = []
    for e in range(plan.cols):
        offsets = [0] * slots
        for flow in range(len(plan.orders)):
            piece, order = plan.pieces[flow], plan.orders[flow]
            inner = plan.span(flow, 0) // piece
            for d in range(plan.fan(flow, 0)):
                for f in range(inner):
                    place = plan.digit(me, order[0]) ^ d
                    rest, size = f, inner
                    for stage in order[1:]:
                        size //= plan.radix[stage]
                        place = place * plan.radix[stage] + (plan.digit(me, stage) ^ (rest // size))
                        rest %= size
                    target = (core ^ e) * plan.half + plan.base(flow) + place * piece
                    copies.append(
                        pltpu.make_async_copy(
                            ins[e * slots + d].at[pl.ds(offsets[d] + f * piece, piece), :],
                            packed.at[pl.ds(pl.multiple_of(target, 8), piece), :],
                            sems.at[len(copies)],
                        )
                    )
                offsets[d] += inner * piece
    trans_copy = pltpu.make_async_copy(trans_hbm, trans_ref, trans_sem)
    for copy in copies:
        copy.start()
    trans_copy.start()
    full_ref[...] = jnp.zeros_like(full_ref)
    for copy in copies:
        copy.wait()

    row_id = lax.broadcasted_iota(jnp.int32, (BLK, BLK), 0)
    col_id = lax.broadcasted_iota(jnp.int32, (BLK, BLK), 1)

    def turned(row):
        return jnp.broadcast_to(row, (BLK, BLK)).T

    corner = plan.tile(0, 0)
    tile = packed[corner : corner + BLK, :]
    hidden = (row_id >= BLK - plan.moment_rows) & (col_id < 64)
    moments = []
    for k in range(nb):
        at = BLK - plan.moment_rows + 2 * k
        moments.append(jnp.concatenate([tile[at : at + 1, 0:64], tile[at + 1 : at + 2, 0:64]], axis=1))
    packed[corner : corner + BLK, :] = jnp.where(hidden, tile.T, tile)

    scales = []
    for k in range(nb):
        row = plan.tile(k, k)
        diagonal = jnp.sum(
            jnp.where(row_id == col_id, packed[row : row + BLK, :], 0.0), axis=0, keepdims=True
        )
        scales.append(lax.rsqrt(diagonal))
        root_ref[k : k + 1, :] = diagonal * scales[k]
        col_ref[k] = turned(scales[k])
    trans_copy.wait()

    def base(k, j):
        if j < nb:
            row = plan.tile(k, j)
            return packed[row : row + BLK, :] * col_ref[k] * scales[j]
        if j < nb + width // BLK:
            at = (j - nb) * BLK
            return trans_ref[at : at + BLK, k * BLK : (k + 1) * BLK].T * col_ref[k]
        return turned(moments[k] * scales[k])

    last = nb + width // BLK

    def lanes_of(tiles):
        return slice(tiles[0] * BLK, (tiles[-1] + 1) * BLK)

    def updated(k, tiles, upto=None):
        value = base(k, tiles[0])
        if len(tiles) > 1:
            value = jnp.concatenate([base(k, j) for j in tiles], axis=1)
        if upto is None:
            upto = k
        if upto:
            rows, done = slice(k * BLK, (k + 1) * BLK), slice(0, upto * BLK)
            value = value - dot3(
                [ref[rows, done] for ref in left], [ref[done, lanes_of(tiles)] for ref in right]
            )
        return value

    def prepare(k, tiles):
        value = updated(k, tiles)
        panel_ref[k % 2, :, lanes_of(tiles)] = value
        if k + 1 < nb and k + 1 in tiles:
            at = tiles.index(k + 1) * BLK
            turn_ref[...] = value[:, at : at + BLK].T

    def prepare_diagonal(k):
        next_ref[...] = updated(k, [k], k - 1)

    def start_next(k, inverse):
        rows, lanes = slice(k * BLK, (k + 1) * BLK), lanes_of([k + 1])
        high, low = split2(panel_ref[k % 2, :, lanes])
        value = dot(inverse, jnp.concatenate([high, low, high], axis=0))
        turned_high, turned_low = split2(turn_ref[...])
        mirror = dot(jnp.concatenate([turned_high, turned_low, turned_high], axis=1), inverse, 1, 1)
        straight, mirrored = split2(value), split2(mirror)
        for part in range(2):
            right[part][rows, lanes] = straight[part]
            left[part][lanes, rows] = mirrored[part]
        full_ref[rows, lanes] = value * root_ref[k + 1 : k + 2, :]
        diagonal = next_ref[...] - dot3(mirrored, straight)
        d_ref[...] = diagonal
        panel_ref[(k + 1) % 2, :, lanes] = diagonal

    z_tile = [None]

    def finish(k, tiles, inverse):
        rows, lanes = slice(k * BLK, (k + 1) * BLK), lanes_of(tiles)
        high, low = split2(panel_ref[k % 2, :, lanes])
        value = dot(inverse, jnp.concatenate([high, low, high], axis=0))
        if k + 1 < nb and tiles[0] > k:
            high, low = split2(value)
            right[0][rows, lanes] = high
            right[1][rows, lanes] = low
        for at, j in enumerate(tiles):
            one = value[:, at * BLK : (at + 1) * BLK]
            if j < nb:
                kept = one * root_ref[j : j + 1, :]
                if j == k:
                    kept = jnp.where(col_id >= row_id, kept, 0.0)
                else:
                    high, low = split2(one.T)
                    left[0][j * BLK : (j + 1) * BLK, rows] = high
                    left[1][j * BLK : (j + 1) * BLK, rows] = low
                full_ref[rows, j * BLK : (j + 1) * BLK] = kept
            elif j < last:
                at_x = (j - nb) * BLK
                part_x = jnp.sum(one * z_tile[0], axis=0, keepdims=True)
                if k:
                    part_x = part_x + x_ref[:, at_x : at_x + BLK]
                x_ref[:, at_x : at_x + BLK] = part_x
            else:
                z_tile[0] = one
                z_all[:, rows] = one.T[0:1, :]

    def groups(first_tile):
        found = [[last]]
        at = first_tile
        while at < last:
            size = 1 if at % 2 or at + 1 >= last or (at < nb <= at + 1) else 2
            found.append(list(range(at, at + size)))
            at += size
        return found

    queue = []
    d_ref[...] = base(0, 0)
    panel_ref[0, :, 0:BLK] = d_ref[...]
    for k in range(nb):
        queue += [functools.partial(prepare, k, tiles) for tiles in groups(k + 1)]
        if k + 1 < nb:
            queue.append(functools.partial(prepare_diagonal, k + 1))
        factor_block(d_ref, inv_ref, cast_ref, times_ref, strip_ref, row_ref, queue)
        inv_high, inv_low = split2(inv_ref[...])
        inverse = jnp.concatenate([inv_high, inv_high, inv_low], axis=1)
        if k + 1 < nb:
            start_next(k, inverse)
        queue += [functools.partial(finish, k, tiles, inverse) for tiles in groups(min(k + 2, nb))]
        queue.append(functools.partial(finish, k, [k], inverse))
    while queue:
        queue.pop(0)()

    rows = pl.ds(pl.multiple_of(me * out_rows, 8), out_rows)
    lanes = pl.ds(pl.multiple_of(core * width, BLK), width)
    r_ref[...] = full_ref[rows, lanes]
    z_ref[...] = z_all[:, lanes]


def per_device(
    whitening,
    sensor_states,
    sensor_coefficients,
    sensor_readings,
    conduit_endpoints,
    conductance,
    balance_right_side,
    prior_root_factor,
    prior_information,
    transition,
):
    n = prior_root_factor.shape[1]
    rows, cols = lax.axis_size("rows"), lax.axis_size("cols")
    plan = Plan(n, rows, cols)
    radix = plan.radix
    params = pltpu.CompilerParams(vmem_limit_bytes=VMEM_LIMIT)
    block_rows, bal_rows = whitening.shape[0], conductance.shape[0]
    depth = block_rows + bal_rows + BLK
    anywhere = pl.BlockSpec(memory_space=pl.ANY)
    hbm = pl.BlockSpec(memory_space=pltpu.HBM)
    vmem = pl.BlockSpec(memory_space=pltpu.VMEM)

    def typed(*shape):
        return jax.ShapeDtypeStruct(shape, F32)

    inputs = (
        whitening,
        sensor_states.T,
        sensor_coefficients.T,
        sensor_readings.reshape(-1, BLK),
        conduit_endpoints.T,
        conductance[None, :],
        balance_right_side[None, :],
        prior_root_factor,
        prior_information[None, :],
    )
    parts = pl.pallas_call(
        functools.partial(assemble_kernel, plan),
        out_shape=[typed(plan.span(f, 0), BLK) for f in range(len(plan.orders)) for _ in range(plan.fan(f, 0))],
        in_specs=[hbm] * len(inputs),
        out_specs=[vmem] * sum(plan.fan(f, 0) for f in range(len(plan.orders))),
        scratch_shapes=[pltpu.VMEM(x.shape, x.dtype) for x in inputs]
        + [
            pltpu.VMEM((n + 16, block_rows), BF16),
            pltpu.VMEM((n + 16, block_rows), BF16),
            pltpu.VMEM((n + 16, depth), BF16),
            pltpu.VMEM((n + 16, depth), BF16),
            pltpu.VMEM((BLK, n), F32),
            pltpu.VMEM((plan.half, BLK), F32),
            pltpu.SemaphoreType.DMA((len(inputs),)),
        ],
        compiler_params=pltpu.CompilerParams(vmem_limit_bytes=WHOLE_VMEM),
        name="assemble",
    )(*inputs)

    def exchange(stage, rel, block):
        flip = rel * plan.stride[stage]
        return lax.ppermute(block, "rows", [(i, i ^ flip) for i in range(rows)])

    steps = len(radix)
    for step in range(steps):
        parts = list(parts)
        got = []
        for flow in range(len(plan.orders)):
            fan, stage = plan.fan(flow, step), plan.orders[flow][step]
            mine = [parts.pop(0) for _ in range(fan)]
            got += mine[:1] + [exchange(stage, d, mine[d]) for d in range(1, fan)]
        last = step + 1 == steps
        shapes = [
            typed(plan.span(flow, step + 1), BLK)
            for flow in range(len(plan.orders))
            for _ in range(1 if last else plan.fan(flow, step + 1))
        ]
        parts = pl.pallas_call(
            functools.partial(sum_kernel, plan, step),
            out_shape=shapes,
            compiler_params=params,
            name="partial_sums",
        )(*got)
    blocks = list(parts)
    for step in reversed(range(steps)):
        got = []
        for flow in range(len(plan.orders)):
            fan, stage = plan.fan(flow, step), plan.orders[flow][step]
            got.append([blocks[flow]] + [exchange(stage, d, blocks[flow]) for d in range(1, fan)])
        if step:
            blocks = [jnp.concatenate(found, axis=0) for found in got]
    swap = [(i, i ^ 1) for i in range(cols)]
    (joined,) = got
    both = joined + [lax.ppermute(block, "cols", swap) for block in joined]

    width = n // cols
    out_rows = n // rows
    wide = n + width + BLK
    r_post, z_post, x_next = pl.pallas_call(
        functools.partial(factor_kernel, plan, out_rows, width),
        out_shape=[typed(out_rows, width), typed(1, width), typed(1, width)],
        in_specs=[anywhere] * (len(both) + 1),
        out_specs=[vmem] * 3,
        scratch_shapes=[
            pltpu.VMEM((cols * plan.half, BLK), F32),
            pltpu.VMEM((BLK, BLK), F32),
            pltpu.VMEM((BLK, BLK), F32),
            pltpu.VMEM((MIC * GRP, BLK), F32),
            pltpu.VMEM((MIC * MIC, BLK), F32),
            pltpu.VMEM((MIC, BLK), F32),
            pltpu.VMEM((MIC, BLK), F32),
            pltpu.VMEM((2, BLK, wide), F32),
            pltpu.VMEM((BLK, BLK), F32),
            pltpu.VMEM((BLK, BLK), F32),
            pltpu.VMEM((n, n), F32),
            pltpu.VMEM((width, n), F32),
            pltpu.VMEM((plan.blocks, BLK, BLK), F32),
            pltpu.VMEM((plan.blocks, BLK), F32),
            pltpu.VMEM((n, n), BF16),
            pltpu.VMEM((n, n), BF16),
            pltpu.VMEM((n, wide), BF16),
            pltpu.VMEM((n, wide), BF16),
            pltpu.VMEM((1, n), F32),
            pltpu.SemaphoreType.DMA((rows * cols,)),
            pltpu.SemaphoreType.DMA,
        ],
        compiler_params=params,
        name="factor",
    )(*both, transition)
    return (r_post, z_post[0], x_next[0])


def solution(mesh):
    in_specs = (
        P("rows", None),
        P("rows", None),
        P("rows", None),
        P("rows"),
        P("rows", None),
        P("rows"),
        P("rows"),
        P("rows", None),
        P("rows"),
        P("cols", None),
    )
    out_specs = (P("rows", "cols"), P("cols"), P("cols"))
    return jax.shard_map(
        per_device, mesh=mesh, in_specs=in_specs, out_specs=out_specs, check_vma=False
    )
```

```python
import functools

import jax
import jax.numpy as jnp
from jax import lax
from jax.experimental import pallas as pl
from jax.experimental.pallas import tpu as pltpu
from jax.sharding import PartitionSpec as P

BLK = 128
MIC = 32
GRP = 8
F32 = jnp.float32
BF16 = jnp.bfloat16
VMEM_LIMIT = 48 * 1024 * 1024
WHOLE_VMEM = 63 * 1024 * 1024


def split2(value):
    high = value.astype(BF16)
    low = (value - high.astype(F32)).astype(BF16)
    return high, low


def dot(left, right, left_dim=1, right_dim=0):
    return lax.dot_general(
        left, right, (((left_dim,), (right_dim,)), ((), ())), preferred_element_type=F32
    )


def dot3(left, right, left_dim=1, right_dim=0):
    total = dot(left[0], right[1], left_dim, right_dim) + dot(left[1], right[0], left_dim, right_dim)
    return total + dot(left[0], right[0], left_dim, right_dim)


def radices(count):
    found = []
    while count > 1:
        found.append(4 if count % 4 == 0 else 2)
        count //= found[-1]
    return tuple(found)


class Plan:
    def __init__(self, state_total, rows, cols):
        self.state_total = state_total
        self.blocks = nb = state_total // BLK
        self.rows, self.cols = rows, cols
        self.radix = radices(rows)
        self.stride = []
        step = 1
        for f in self.radix:
            self.stride.append(step)
            step *= f
        stages = list(range(len(self.radix)))
        self.orders = (stages,)
        tiles = [(i, j) for i in range(nb) for j in range(i, nb)]
        share = -(-len(tiles) // cols)
        piece = -(-share * BLK // (8 * rows)) * 8
        self.pieces = (piece,)
        self.half = rows * piece
        self.local = {}
        for index, tile in enumerate(tiles):
            self.local[tile] = (index // share, index % share * BLK)
        self.moment_rows = state_total // 64

    def tile(self, i, j):
        core, row = self.local[i, j]
        return core * self.half + row

    def digit(self, index, stage):
        return lax.rem(index // self.stride[stage], self.radix[stage])

    def base(self, flow):
        return self.rows * self.pieces[0] * flow

    def span(self, flow, step):
        size = self.pieces[flow]
        for stage in self.orders[flow][step + 1 :]:
            size *= self.radix[stage]
        return size

    def fan(self, flow, step):
        return self.radix[self.orders[flow][step]]


def assemble_kernel(plan, *refs):
    fans = [plan.fan(flow, 0) for flow in range(len(plan.orders))]
    ins, outs, scratch = refs[:9], refs[9 : 9 + sum(fans)], refs[9 + sum(fans) :]
    here, (sens_hi, sens_lo, at_hi, at_lo, prior_pad, packed, sems) = scratch[:9], scratch[9:]
    copies = [pltpu.make_async_copy(a, b, sems.at[i]) for i, (a, b) in enumerate(zip(ins, here))]
    for copy in copies:
        copy.start()
    (
        white_ref,
        states_ref,
        coeffs_ref,
        readings_ref,
        ends_ref,
        conductance_ref,
        balance_rhs_ref,
        prior_ref,
        prior_info_ref,
    ) = here
    n = plan.state_total
    block_rows = white_ref.shape[0]
    bal_rows = conductance_ref.shape[1]
    prior_rows = prior_ref.shape[0]
    head = 16
    step = 64

    def put(high_ref, low_ref, row, col, value):
        high, low = split2(value)
        high_ref[row : row + value.shape[0], col : col + value.shape[1]] = high
        low_ref[row : row + value.shape[0], col : col + value.shape[1]] = low

    def head_rows(row):
        top = lax.broadcasted_iota(jnp.int32, (head, row.shape[1]), 0) == 0
        return jnp.where(top, jnp.broadcast_to(row, (head, row.shape[1])), 0.0)

    prior_pad[...] = jnp.zeros_like(prior_pad)
    used = max(row for _, row in plan.local.values()) + BLK
    if used < plan.half:
        packed[used:, :] = jnp.zeros((plan.half - used, BLK), F32)
    for copy in copies:
        copy.wait()

    readings = jnp.concatenate(
        [readings_ref[k : k + 1, :] for k in range(readings_ref.shape[0])], axis=1
    )
    put(sens_hi, sens_lo, 0, 0, head_rows(readings))
    for at in range(0, n, step):
        ids = lax.broadcasted_iota(jnp.int32, (step, block_rows), 0) + at
        summed = jnp.zeros((step, block_rows), F32)
        for k in range(states_ref.shape[0]):
            summed = summed + jnp.where(ids == states_ref[k : k + 1, :], coeffs_ref[k : k + 1, :], 0.0)
        put(sens_hi, sens_lo, head + at, 0, summed)
    white = split2(white_ref[...])
    whitened = dot3((sens_hi[...], sens_lo[...]), white, 1, 1)
    for at in range(0, n + head, step):
        size = min(step, n + head - at)
        put(at_hi, at_lo, at, 0, whitened[at : at + size, :])

    conductance = conductance_ref[...]
    put(at_hi, at_lo, 0, block_rows, head_rows(conductance * balance_rhs_ref[...]))
    for at in range(0, n, step):
        ids = lax.broadcasted_iota(jnp.int32, (step, bal_rows), 0) + at
        value = jnp.where(ids == ends_ref[0:1, :], conductance, 0.0)
        value = value + jnp.where(ids == ends_ref[1:2, :], -conductance, 0.0)
        put(at_hi, at_lo, head + at, block_rows, value)

    prior_col = block_rows + bal_rows
    prior_pad[0:prior_rows, :] = prior_ref[...]
    info = jnp.concatenate([prior_info_ref[...], jnp.zeros((1, BLK - prior_rows), F32)], axis=1)
    put(at_hi, at_lo, 0, prior_col, head_rows(info))
    for at in range(0, n, BLK):
        put(at_hi, at_lo, head + at, prior_col, prior_pad[:, at : at + BLK].T)

    me, core = lax.axis_index("rows"), lax.axis_index("cols")

    def tiles_of(part):
        moments = []
        for at in range(0, plan.blocks, 2):
            wanted = [(i, j) for (i, j), (c, _) in plan.local.items() if c == part and j // 2 == at // 2]
            if not wanted:
                continue
            low, high = min(i for i, _ in wanted), max(i for i, _ in wanted) + 1
            top = head + low * BLK if low else 0
            rows = slice(top, head + high * BLK)
            cols = slice(head + at * BLK, head + (at + 2) * BLK)
            out = dot3((at_hi[rows, :], at_lo[rows, :]), (at_hi[cols, :], at_lo[cols, :]), 1, 1)
            if not low:
                moments += [out[0:1, k * 64 : k * 64 + 64] for k in range(2 * BLK // 64)]
            for i, j in wanted:
                row, col = plan.local[i, j][1], (j - at) * BLK
                where = head + i * BLK - top
                packed[row : row + BLK, :] = out[where : where + BLK, col : col + BLK]
        for k, value in enumerate(moments):
            row = plan.local[0, 0][1] + BLK - plan.moment_rows + k
            packed[row : row + 1, 0:64] = value

    for part in range(plan.cols):
        pl.when(core == part)(functools.partial(tiles_of, part))

    outs = list(outs)
    for flow in range(len(plan.orders)):
        span, stage = plan.span(flow, 0), plan.orders[flow][0]
        for d in range(fans[flow]):
            at = plan.base(flow) + (plan.digit(me, stage) ^ d) * span
            outs.pop(0)[...] = packed[pl.ds(pl.multiple_of(at, 8), span), :]


def sum_kernel(plan, step, *refs):
    me = lax.axis_index("rows")
    refs = list(refs)
    ins = [[refs.pop(0) for _ in range(plan.fan(flow, step))] for flow in range(len(plan.orders))]
    last = step + 1 == len(plan.radix)
    for flow in range(len(plan.orders)):
        count = 1 if last else plan.fan(flow, step + 1)
        span = plan.span(flow, step + 1)
        for d in range(count):
            at = 0 if last else (plan.digit(me, plan.orders[flow][step + 1]) ^ d) * span
            rows = pl.ds(pl.multiple_of(at, 8), span)
            total = ins[flow][0][rows, :]
            for other in ins[flow][1:]:
                total = total + other[rows, :]
            refs.pop(0)[...] = total


def eliminate(s, rows):
    u = [[None] * GRP for _ in range(GRP)]
    pairs, done = [], []
    for p in range(0, GRP, 2):
        a, b, c = s[p][p], s[p + 1][p], s[p + 1][p + 1]
        det = a * c - b * b
        root_det = lax.rsqrt(det)
        root_a = lax.rsqrt(a)
        second = root_a * root_det
        inv = root_det * root_det
        u[p + 1][p] = b * root_a
        left = {}
        for i in range(p + 2, GRP):
            one, two = s[i][p], s[i][p + 1]
            cross = a * two - b * one
            left[i] = (c * one - b * two, cross)
            u[i][p] = one * root_a
            u[i][p + 1] = cross * second
        for c_at in range(p + 2, GRP):
            for i in range(c_at, GRP):
                fall = left[i][0] * s[c_at][p] + left[i][1] * s[c_at][p + 1]
                s[i][c_at] = s[i][c_at] - fall * inv
        pairs.append((a, b, root_a, second))
        done.append(rows[p] * root_a)
        done.append((a * rows[p + 1] - b * rows[p]) * second)
        for i in range(p + 2, GRP):
            rows[i] = rows[i] - (u[i][p] * done[p] + u[i][p + 1] * done[p + 1])
    return u, pairs, done


def factor_block(d_ref, inv_ref, cast_ref, times_ref, strip_ref, row_ref, queue):
    lane = lax.broadcasted_iota(jnp.int32, (MIC, BLK), 1)
    sub = lax.broadcasted_iota(jnp.int32, (MIC, BLK), 0)
    groups = MIC // GRP
    slots = groups * (BLK // MIC)
    share = -(-len(queue) // slots)

    def background():
        for _ in range(min(share, len(queue))):
            queue.pop(0)()

    for m in range(BLK // MIC):
        r0 = m * MIC
        strip = d_ref[r0 : r0 + MIC, :]
        inside = (lane >= r0) & (lane < r0 + MIC)
        ready = jnp.where(inside, jnp.where(lane == r0 + sub, 1.0, 0.0), strip)
        low, rest = [], []
        for g in range(groups):
            part = strip[g * GRP : (g + 1) * GRP, :]
            low.append(
                [
                    jnp.broadcast_to(part[:, r0 + c : r0 + c + 1], (GRP, BLK))
                    for c in range((g + 1) * GRP)
                ]
            )
            rest.append(ready[g * GRP : (g + 1) * GRP, :])
        for s in range(groups):
            base = s * GRP * GRP
            for c in range(GRP):
                cast_ref[base + GRP * c : base + GRP * (c + 1), :] = low[s][s * GRP + c]
            strip_ref[s * GRP : (s + 1) * GRP, :] = rest[s]
            splats = [
                [
                    cast_ref[base + GRP * c + i : base + GRP * c + i + 1, :] if i >= c else None
                    for c in range(GRP)
                ]
                for i in range(GRP)
            ]
            background()
            u, pairs, done = eliminate(
                splats, [strip_ref[s * GRP + i : s * GRP + i + 1, :] for i in range(GRP)]
            )
            for j in range(GRP):
                row_ref[s * GRP + j : s * GRP + j + 1, :] = done[j]
            for g in range(s + 1, groups):
                mine = low[g][s * GRP : (s + 1) * GRP]
                for p in range(0, GRP, 2):
                    a, b, root_a, second = pairs[p // 2]
                    one, two = mine[p], mine[p + 1]
                    mine[p] = one * root_a
                    mine[p + 1] = (a * two - b * one) * second
                    for c in range(p + 2, GRP):
                        mine[c] = mine[c] - (mine[p] * u[c][p] + mine[p + 1] * u[c][p + 1])
                times = (s * groups + g) * GRP * GRP
                for j in range(GRP):
                    times_ref[times + GRP * j : times + GRP * (j + 1), :] = mine[j]
                    rest[g] = rest[g] - mine[j] * done[j]
                for h in range(s + 1, g + 1):
                    other = (s * groups + h) * GRP * GRP
                    for c in range(GRP):
                        total = low[g][h * GRP + c]
                        for j in range(0, GRP, 2):
                            at = other + GRP * j + c
                            total = total - (
                                mine[j] * times_ref[at : at + 1, :]
                                + mine[j + 1] * times_ref[at + GRP : at + GRP + 1, :]
                            )
                        low[g][h * GRP + c] = total
        solved = row_ref[...]
        inv_ref[r0 : r0 + MIC, :] = jnp.where(lane < r0 + MIC, solved, 0.0)
        if r0 + MIC < BLK:
            high, low_part = split2(solved)
            fix = dot(
                jnp.concatenate([high, high, low_part], axis=0),
                jnp.concatenate([high, low_part, high], axis=0),
                0,
                0,
            )
            lanes = lax.broadcasted_iota(jnp.int32, (BLK - r0 - MIC, BLK), 1)
            keep = (lanes < r0) | (lanes >= r0 + MIC)
            left = jnp.where(keep, d_ref[r0 + MIC :, :], 0.0)
            d_ref[r0 + MIC :, :] = left - fix[r0 + MIC :, :]
    while queue:
        queue.pop(0)()


def factor_kernel(plan, out_rows, width, *refs):
    n, nb = plan.state_total, plan.blocks
    slots = max(plan.fan(flow, 0) for flow in range(len(plan.orders)))
    ins, (trans_ref, r_ref, z_ref, x_ref, *scratch) = refs[: slots * plan.cols], refs[slots * plan.cols :]
    (
        packed,
        d_ref,
        inv_ref,
        cast_ref,
        times_ref,
        strip_ref,
        row_ref,
        panel_ref,
        turn_ref,
        next_ref,
        full_ref,
        col_ref,
        root_ref,
        *state,
    ) = scratch
    left, right, z_all = state[:2], state[2:4], state[4]
    me, core = lax.axis_index("rows"), lax.axis_index("cols")

    for e in range(plan.cols):
        offsets = [0] * slots
        for flow in range(len(plan.orders)):
            piece, order = plan.pieces[flow], plan.orders[flow]
            inner = plan.span(flow, 0) // piece
            for d in range(plan.fan(flow, 0)):
                for f in range(inner):
                    place = plan.digit(me, order[0]) ^ d
                    rest, size = f, inner
                    for stage in order[1:]:
                        size //= plan.radix[stage]
                        place = place * plan.radix[stage] + (plan.digit(me, stage) ^ (rest // size))
                        rest %= size
                    target = (core ^ e) * plan.half + plan.base(flow) + place * piece
                    at = offsets[d] + f * piece
                    packed[pl.ds(pl.multiple_of(target, 8), piece), :] = ins[e * slots + d][
                        at : at + piece, :
                    ]
                offsets[d] += inner * piece
    full_ref[...] = jnp.zeros_like(full_ref)

    row_id = lax.broadcasted_iota(jnp.int32, (BLK, BLK), 0)
    col_id = lax.broadcasted_iota(jnp.int32, (BLK, BLK), 1)

    def turned(row):
        return jnp.broadcast_to(row, (BLK, BLK)).T

    corner = plan.tile(0, 0)
    tile = packed[corner : corner + BLK, :]
    hidden = (row_id >= BLK - plan.moment_rows) & (col_id < 64)
    moments = []
    for k in range(nb):
        at = BLK - plan.moment_rows + 2 * k
        moments.append(jnp.concatenate([tile[at : at + 1, 0:64], tile[at + 1 : at + 2, 0:64]], axis=1))
    packed[corner : corner + BLK, :] = jnp.where(hidden, tile.T, tile)

    scales = []
    for k in range(nb):
        row = plan.tile(k, k)
        diagonal = jnp.sum(
            jnp.where(row_id == col_id, packed[row : row + BLK, :], 0.0), axis=0, keepdims=True
        )
        scales.append(lax.rsqrt(diagonal))
        root_ref[k : k + 1, :] = diagonal * scales[k]
        col_ref[k] = turned(scales[k])

    def base(k, j):
        if j < nb:
            row = plan.tile(k, j)
            return packed[row : row + BLK, :] * col_ref[k] * scales[j]
        if j < nb + width // BLK:
            at = (j - nb) * BLK
            return trans_ref[at : at + BLK, k * BLK : (k + 1) * BLK].T * col_ref[k]
        return turned(moments[k] * scales[k])

    last = nb + width // BLK

    def lanes_of(tiles):
        return slice(tiles[0] * BLK, (tiles[-1] + 1) * BLK)

    def updated(k, tiles, upto=None):
        value = base(k, tiles[0])
        if len(tiles) > 1:
            value = jnp.concatenate([base(k, j) for j in tiles], axis=1)
        if upto is None:
            upto = k
        if upto:
            rows, done = slice(k * BLK, (k + 1) * BLK), slice(0, upto * BLK)
            value = value - dot3(
                [ref[rows, done] for ref in left], [ref[done, lanes_of(tiles)] for ref in right]
            )
        return value

    def prepare(k, tiles):
        value = updated(k, tiles)
        panel_ref[k % 2, :, lanes_of(tiles)] = value
        if k + 1 < nb and k + 1 in tiles:
            at = tiles.index(k + 1) * BLK
            turn_ref[...] = value[:, at : at + BLK].T

    def prepare_diagonal(k):
        next_ref[...] = updated(k, [k], k - 1)

    def start_next(k, inverse):
        rows, lanes = slice(k * BLK, (k + 1) * BLK), lanes_of([k + 1])
        high, low = split2(panel_ref[k % 2, :, lanes])
        value = dot(inverse, jnp.concatenate([high, low, high], axis=0))
        turned_high, turned_low = split2(turn_ref[...])
        mirror = dot(jnp.concatenate([turned_high, turned_low, turned_high], axis=1), inverse, 1, 1)
        straight, mirrored = split2(value), split2(mirror)
        for part in range(2):
            right[part][rows, lanes] = straight[part]
            left[part][lanes, rows] = mirrored[part]
        full_ref[rows, lanes] = value * root_ref[k + 1 : k + 2, :]
        diagonal = next_ref[...] - dot3(mirrored, straight)
        d_ref[...] = diagonal
        panel_ref[(k + 1) % 2, :, lanes] = diagonal

    z_tile = [None]

    def finish(k, tiles, inverse):
        rows, lanes = slice(k * BLK, (k + 1) * BLK), lanes_of(tiles)
        high, low = split2(panel_ref[k % 2, :, lanes])
        value = dot(inverse, jnp.concatenate([high, low, high], axis=0))
        if k + 1 < nb and tiles[0] > k:
            high, low = split2(value)
            right[0][rows, lanes] = high
            right[1][rows, lanes] = low
        for at, j in enumerate(tiles):
            one = value[:, at * BLK : (at + 1) * BLK]
            if j < nb:
                kept = one * root_ref[j : j + 1, :]
                if j == k:
                    kept = jnp.where(col_id >= row_id, kept, 0.0)
                else:
                    high, low = split2(one.T)
                    left[0][j * BLK : (j + 1) * BLK, rows] = high
                    left[1][j * BLK : (j + 1) * BLK, rows] = low
                full_ref[rows, j * BLK : (j + 1) * BLK] = kept
            elif j < last:
                at_x = (j - nb) * BLK
                part_x = jnp.sum(one * z_tile[0], axis=0, keepdims=True)
                if k:
                    part_x = part_x + x_ref[:, at_x : at_x + BLK]
                x_ref[:, at_x : at_x + BLK] = part_x
            else:
                z_tile[0] = one
                z_all[:, rows] = one.T[0:1, :]

    def groups(first_tile):
        found = [[last]]
        at = first_tile
        while at < last:
            size = 1 if at % 2 or at + 1 >= last or (at < nb <= at + 1) else 2
            found.append(list(range(at, at + size)))
            at += size
        return found

    queue = []
    d_ref[...] = base(0, 0)
    panel_ref[0, :, 0:BLK] = d_ref[...]
    for k in range(nb):
        queue += [functools.partial(prepare, k, tiles) for tiles in groups(k + 1)]
        if k + 1 < nb:
            queue.append(functools.partial(prepare_diagonal, k + 1))
        factor_block(d_ref, inv_ref, cast_ref, times_ref, strip_ref, row_ref, queue)
        inv_high, inv_low = split2(inv_ref[...])
        inverse = jnp.concatenate([inv_high, inv_high, inv_low], axis=1)
        if k + 1 < nb:
            start_next(k, inverse)
        queue += [functools.partial(finish, k, tiles, inverse) for tiles in groups(min(k + 2, nb))]
        queue.append(functools.partial(finish, k, [k], inverse))
    while queue:
        queue.pop(0)()

    rows = pl.ds(pl.multiple_of(me * out_rows, 8), out_rows)
    lanes = pl.ds(pl.multiple_of(core * width, BLK), width)
    r_ref[...] = full_ref[rows, lanes]
    z_ref[...] = z_all[:, lanes]


def per_device(
    whitening,
    sensor_states,
    sensor_coefficients,
    sensor_readings,
    conduit_endpoints,
    conductance,
    balance_right_side,
    prior_root_factor,
    prior_information,
    transition,
):
    n = prior_root_factor.shape[1]
    rows, cols = lax.axis_size("rows"), lax.axis_size("cols")
    plan = Plan(n, rows, cols)
    radix = plan.radix
    params = pltpu.CompilerParams(vmem_limit_bytes=VMEM_LIMIT)
    block_rows, bal_rows = whitening.shape[0], conductance.shape[0]
    depth = block_rows + bal_rows + BLK
    hbm = pl.BlockSpec(memory_space=pltpu.HBM)
    vmem = pl.BlockSpec(memory_space=pltpu.VMEM)

    def typed(*shape):
        return jax.ShapeDtypeStruct(shape, F32)

    inputs = (
        whitening,
        sensor_states.T,
        sensor_coefficients.T,
        sensor_readings.reshape(-1, BLK),
        conduit_endpoints.T,
        conductance[None, :],
        balance_right_side[None, :],
        prior_root_factor,
        prior_information[None, :],
    )
    parts = pl.pallas_call(
        functools.partial(assemble_kernel, plan),
        out_shape=[typed(plan.span(f, 0), BLK) for f in range(len(plan.orders)) for _ in range(plan.fan(f, 0))],
        in_specs=[hbm] * len(inputs),
        out_specs=[vmem] * sum(plan.fan(f, 0) for f in range(len(plan.orders))),
        scratch_shapes=[pltpu.VMEM(x.shape, x.dtype) for x in inputs]
        + [
            pltpu.VMEM((n + 16, block_rows), BF16),
            pltpu.VMEM((n + 16, block_rows), BF16),
            pltpu.VMEM((n + 16, depth), BF16),
            pltpu.VMEM((n + 16, depth), BF16),
            pltpu.VMEM((BLK, n), F32),
            pltpu.VMEM((plan.half, BLK), F32),
            pltpu.SemaphoreType.DMA((len(inputs),)),
        ],
        compiler_params=pltpu.CompilerParams(vmem_limit_bytes=WHOLE_VMEM),
        name="assemble",
    )(*inputs)

    def exchange(stage, rel, block):
        flip = rel * plan.stride[stage]
        return lax.ppermute(block, "rows", [(i, i ^ flip) for i in range(rows)])

    steps = len(radix)
    for step in range(steps):
        parts = list(parts)
        got = []
        for flow in range(len(plan.orders)):
            fan, stage = plan.fan(flow, step), plan.orders[flow][step]
            mine = [parts.pop(0) for _ in range(fan)]
            got += mine[:1] + [exchange(stage, d, mine[d]) for d in range(1, fan)]
        last = step + 1 == steps
        shapes = [
            typed(plan.span(flow, step + 1), BLK)
            for flow in range(len(plan.orders))
            for _ in range(1 if last else plan.fan(flow, step + 1))
        ]
        parts = pl.pallas_call(
            functools.partial(sum_kernel, plan, step),
            out_shape=shapes,
            compiler_params=params,
            name="partial_sums",
        )(*got)
    blocks = list(parts)
    for step in reversed(range(steps)):
        got = []
        for flow in range(len(plan.orders)):
            fan, stage = plan.fan(flow, step), plan.orders[flow][step]
            got.append([blocks[flow]] + [exchange(stage, d, blocks[flow]) for d in range(1, fan)])
        if step:
            blocks = [jnp.concatenate(found, axis=0) for found in got]
    swap = [(i, i ^ 1) for i in range(cols)]
    (joined,) = got
    both = joined + [lax.ppermute(block, "cols", swap) for block in joined]

    width = n // cols
    out_rows = n // rows
    wide = n + width + BLK
    r_post, z_post, x_next = pl.pallas_call(
        functools.partial(factor_kernel, plan, out_rows, width),
        out_shape=[typed(out_rows, width), typed(1, width), typed(1, width)],
        in_specs=[vmem] * (len(both) + 1),
        out_specs=[vmem] * 3,
        scratch_shapes=[
            pltpu.VMEM((cols * plan.half, BLK), F32),
            pltpu.VMEM((BLK, BLK), F32),
            pltpu.VMEM((BLK, BLK), F32),
            pltpu.VMEM((MIC * GRP, BLK), F32),
            pltpu.VMEM((MIC * MIC, BLK), F32),
            pltpu.VMEM((MIC, BLK), F32),
            pltpu.VMEM((MIC, BLK), F32),
            pltpu.VMEM((2, BLK, wide), F32),
            pltpu.VMEM((BLK, BLK), F32),
            pltpu.VMEM((BLK, BLK), F32),
            pltpu.VMEM((n, n), F32),
            pltpu.VMEM((plan.blocks, BLK, BLK), F32),
            pltpu.VMEM((plan.blocks, BLK), F32),
            pltpu.VMEM((n, n), BF16),
            pltpu.VMEM((n, n), BF16),
            pltpu.VMEM((n, wide), BF16),
            pltpu.VMEM((n, wide), BF16),
            pltpu.VMEM((1, n), F32),
        ],
        compiler_params=params,
        name="factor",
    )(*both, transition)
    return (r_post, z_post[0], x_next[0])


def solution(mesh):
    in_specs = (
        P("rows", None),
        P("rows", None),
        P("rows", None),
        P("rows"),
        P("rows", None),
        P("rows"),
        P("rows"),
        P("rows", None),
        P("rows"),
        P("cols", None),
    )
    out_specs = (P("rows", "cols"), P("cols"), P("cols"))
    return jax.shard_map(
        per_device, mesh=mesh, in_specs=in_specs, out_specs=out_specs, check_vma=False
    )
```

```python
import functools

import jax
import jax.numpy as jnp
from jax import lax
from jax.experimental import pallas as pl
from jax.experimental.pallas import tpu as pltpu
from jax.sharding import PartitionSpec as P

BLK = 128
MIC = 32
GRP = 8
F32 = jnp.float32
BF16 = jnp.bfloat16
VMEM_LIMIT = 48 * 1024 * 1024
WHOLE_VMEM = 63 * 1024 * 1024


def split2(value):
    high = value.astype(BF16)
    low = (value - high.astype(F32)).astype(BF16)
    return high, low


def dot(left, right, left_dim=1, right_dim=0):
    return lax.dot_general(
        left, right, (((left_dim,), (right_dim,)), ((), ())), preferred_element_type=F32
    )


def dot3(left, right, left_dim=1, right_dim=0):
    total = dot(left[0], right[1], left_dim, right_dim) + dot(left[1], right[0], left_dim, right_dim)
    return total + dot(left[0], right[0], left_dim, right_dim)


def radices(count):
    found = []
    while count > 1:
        found.append(4 if count % 4 == 0 else 2)
        count //= found[-1]
    return tuple(found)


class Plan:
    def __init__(self, state_total, rows, cols):
        self.state_total = state_total
        self.blocks = nb = state_total // BLK
        self.rows, self.cols = rows, cols
        self.radix = radices(rows)
        self.stride = []
        step = 1
        for f in self.radix:
            self.stride.append(step)
            step *= f
        stages = list(range(len(self.radix)))
        self.orders = (stages,)
        tiles = [(i, j) for i in range(nb) for j in range(i, nb) if i != j or i % 2 == 0]
        share = -(-len(tiles) // cols)
        self.extra = share * BLK
        piece = -(-(self.extra + nb + nb // 2) // (8 * rows)) * 8
        self.pieces = (piece,)
        self.half = rows * piece
        self.local = {}
        for index, tile in enumerate(tiles):
            self.local[tile] = (index // share, index % share * BLK)

    def tile(self, i, j):
        core, row = self.local[i, j]
        return core * self.half + row

    def diagonal_row(self, k):
        return self.local[k - 1, k - 1][0] * self.half + self.extra + self.blocks + k // 2

    def digit(self, index, stage):
        return lax.rem(index // self.stride[stage], self.radix[stage])

    def base(self, flow):
        return self.rows * self.pieces[0] * flow

    def span(self, flow, step):
        size = self.pieces[flow]
        for stage in self.orders[flow][step + 1 :]:
            size *= self.radix[stage]
        return size

    def fan(self, flow, step):
        return self.radix[self.orders[flow][step]]


def assemble_kernel(plan, *refs):
    fans = [plan.fan(flow, 0) for flow in range(len(plan.orders))]
    ins, outs, scratch = refs[:9], refs[9 : 9 + sum(fans)], refs[9 + sum(fans) :]
    here, (sens_hi, sens_lo, at_hi, at_lo, prior_pad, packed, sems) = scratch[:9], scratch[9:]
    copies = [pltpu.make_async_copy(a, b, sems.at[i]) for i, (a, b) in enumerate(zip(ins, here))]
    for copy in copies:
        copy.start()
    (
        white_ref,
        states_ref,
        coeffs_ref,
        readings_ref,
        ends_ref,
        conductance_ref,
        balance_rhs_ref,
        prior_ref,
        prior_info_ref,
    ) = here
    n = plan.state_total
    block_rows = white_ref.shape[0]
    bal_rows = conductance_ref.shape[1]
    prior_rows = prior_ref.shape[0]
    head = 16
    step = 64

    def put(high_ref, low_ref, row, col, value):
        high, low = split2(value)
        high_ref[row : row + value.shape[0], col : col + value.shape[1]] = high
        low_ref[row : row + value.shape[0], col : col + value.shape[1]] = low

    def head_rows(row):
        top = lax.broadcasted_iota(jnp.int32, (head, row.shape[1]), 0) == 0
        return jnp.where(top, jnp.broadcast_to(row, (head, row.shape[1])), 0.0)

    prior_pad[...] = jnp.zeros_like(prior_pad)
    packed[plan.extra :, :] = jnp.zeros((plan.half - plan.extra, BLK), F32)
    for index in (1, 2, 3):
        copies[index].wait()

    readings = jnp.concatenate(
        [readings_ref[k : k + 1, :] for k in range(readings_ref.shape[0])], axis=1
    )
    put(sens_hi, sens_lo, 0, 0, head_rows(readings))
    for at in range(0, n, step):
        ids = lax.broadcasted_iota(jnp.int32, (step, block_rows), 0) + at
        summed = jnp.zeros((step, block_rows), F32)
        for k in range(states_ref.shape[0]):
            summed = summed + jnp.where(ids == states_ref[k : k + 1, :], coeffs_ref[k : k + 1, :], 0.0)
        put(sens_hi, sens_lo, head + at, 0, summed)
    copies[0].wait()
    white = split2(white_ref[...])
    whitened = dot3((sens_hi[...], sens_lo[...]), white, 1, 1)
    for at in range(0, n + head, step):
        size = min(step, n + head - at)
        put(at_hi, at_lo, at, 0, whitened[at : at + size, :])

    for copy in copies[4:]:
        copy.wait()
    conductance = conductance_ref[...]
    put(at_hi, at_lo, 0, block_rows, head_rows(conductance * balance_rhs_ref[...]))
    for at in range(0, n, step):
        ids = lax.broadcasted_iota(jnp.int32, (step, bal_rows), 0) + at
        value = jnp.where(ids == ends_ref[0:1, :], conductance, 0.0)
        value = value + jnp.where(ids == ends_ref[1:2, :], -conductance, 0.0)
        put(at_hi, at_lo, head + at, block_rows, value)

    prior_col = block_rows + bal_rows
    prior_pad[0:prior_rows, :] = prior_ref[...]
    info = jnp.concatenate([prior_info_ref[...], jnp.zeros((1, BLK - prior_rows), F32)], axis=1)
    put(at_hi, at_lo, 0, prior_col, head_rows(info))
    for at in range(0, n, BLK):
        put(at_hi, at_lo, head + at, prior_col, prior_pad[:, at : at + BLK].T)

    me, core = lax.axis_index("rows"), lax.axis_index("cols")

    row_id = lax.broadcasted_iota(jnp.int32, (BLK, BLK), 0)
    col_id = lax.broadcasted_iota(jnp.int32, (BLK, BLK), 1)

    def tiles_of(part):
        for at in range(0, plan.blocks, 2):
            wanted = [(i, j) for (i, j), (c, _) in plan.local.items() if c == part and j // 2 == at // 2]
            if not wanted:
                continue
            low = min(i for i, _ in wanted)
            high = max(i + (i == j) for i, j in wanted) + 1
            top = head + low * BLK if low else 0
            rows = slice(top, head + high * BLK)
            cols = slice(head + at * BLK, head + (at + 2) * BLK)
            out = dot3((at_hi[rows, :], at_lo[rows, :]), (at_hi[cols, :], at_lo[cols, :]), 1, 1)

            def piece_of(i, j):
                where, col = head + i * BLK - top, (j - at) * BLK
                return out[where : where + BLK, col : col + BLK]

            if part == 0:
                for j in (at, at + 1):
                    col = (j - at) * BLK
                    packed[plan.extra + j : plan.extra + j + 1, :] = out[0:1, col : col + BLK]
            for i, j in wanted:
                row = plan.local[i, j][1]
                value = piece_of(i, j)
                if i == j:
                    second = piece_of(i + 1, j + 1)
                    spare = plan.extra + plan.blocks + i // 2
                    packed[spare : spare + 1, :] = jnp.sum(
                        jnp.where(row_id == col_id, second, 0.0), axis=0, keepdims=True
                    )
                    value = jnp.where(col_id >= row_id, value, second)
                packed[row : row + BLK, :] = value

    for part in range(plan.cols):
        pl.when(core == part)(functools.partial(tiles_of, part))

    outs = list(outs)
    for flow in range(len(plan.orders)):
        span, stage = plan.span(flow, 0), plan.orders[flow][0]
        for d in range(fans[flow]):
            at = plan.base(flow) + (plan.digit(me, stage) ^ d) * span
            outs.pop(0)[...] = packed[pl.ds(pl.multiple_of(at, 8), span), :]


def sum_kernel(plan, step, *refs):
    me = lax.axis_index("rows")
    refs = list(refs)
    ins = [[refs.pop(0) for _ in range(plan.fan(flow, step))] for flow in range(len(plan.orders))]
    last = step + 1 == len(plan.radix)
    for flow in range(len(plan.orders)):
        count = 1 if last else plan.fan(flow, step + 1)
        span = plan.span(flow, step + 1)
        for d in range(count):
            at = 0 if last else (plan.digit(me, plan.orders[flow][step + 1]) ^ d) * span
            rows = pl.ds(pl.multiple_of(at, 8), span)
            total = ins[flow][0][rows, :]
            for other in ins[flow][1:]:
                total = total + other[rows, :]
            refs.pop(0)[...] = total


def eliminate(s, rows):
    u = [[None] * GRP for _ in range(GRP)]
    pairs, done = [], []
    for p in range(0, GRP, 2):
        a, b, c = s[p][p], s[p + 1][p], s[p + 1][p + 1]
        det = a * c - b * b
        root_det = lax.rsqrt(det)
        root_a = lax.rsqrt(a)
        second = root_a * root_det
        inv = root_det * root_det
        u[p + 1][p] = b * root_a
        left = {}
        for i in range(p + 2, GRP):
            one, two = s[i][p], s[i][p + 1]
            cross = a * two - b * one
            left[i] = (c * one - b * two, cross)
            u[i][p] = one * root_a
            u[i][p + 1] = cross * second
        for c_at in range(p + 2, GRP):
            for i in range(c_at, GRP):
                fall = left[i][0] * s[c_at][p] + left[i][1] * s[c_at][p + 1]
                s[i][c_at] = s[i][c_at] - fall * inv
        pairs.append((a, b, root_a, second))
        done.append(rows[p] * root_a)
        done.append((a * rows[p + 1] - b * rows[p]) * second)
        for i in range(p + 2, GRP):
            rows[i] = rows[i] - (u[i][p] * done[p] + u[i][p + 1] * done[p + 1])
    return u, pairs, done


def factor_block(d_ref, inv_ref, cast_ref, times_ref, strip_ref, row_ref, queue):
    lane = lax.broadcasted_iota(jnp.int32, (MIC, BLK), 1)
    sub = lax.broadcasted_iota(jnp.int32, (MIC, BLK), 0)
    groups = MIC // GRP
    slots = groups * (BLK // MIC)
    share = -(-len(queue) // slots)

    def background():
        for _ in range(min(share, len(queue))):
            queue.pop(0)()

    for m in range(BLK // MIC):
        r0 = m * MIC
        strip = d_ref[r0 : r0 + MIC, :]
        inside = (lane >= r0) & (lane < r0 + MIC)
        ready = jnp.where(inside, jnp.where(lane == r0 + sub, 1.0, 0.0), strip)
        low, rest = [], []
        for g in range(groups):
            part = strip[g * GRP : (g + 1) * GRP, :]
            low.append(
                [
                    jnp.broadcast_to(part[:, r0 + c : r0 + c + 1], (GRP, BLK))
                    for c in range((g + 1) * GRP)
                ]
            )
            rest.append(ready[g * GRP : (g + 1) * GRP, :])
        for s in range(groups):
            base = s * GRP * GRP
            for c in range(GRP):
                cast_ref[base + GRP * c : base + GRP * (c + 1), :] = low[s][s * GRP + c]
            strip_ref[s * GRP : (s + 1) * GRP, :] = rest[s]
            splats = [
                [
                    cast_ref[base + GRP * c + i : base + GRP * c + i + 1, :] if i >= c else None
                    for c in range(GRP)
                ]
                for i in range(GRP)
            ]
            background()
            u, pairs, done = eliminate(
                splats, [strip_ref[s * GRP + i : s * GRP + i + 1, :] for i in range(GRP)]
            )
            for j in range(GRP):
                row_ref[s * GRP + j : s * GRP + j + 1, :] = done[j]
            for g in range(s + 1, groups):
                mine = low[g][s * GRP : (s + 1) * GRP]
                for p in range(0, GRP, 2):
                    a, b, root_a, second = pairs[p // 2]
                    one, two = mine[p], mine[p + 1]
                    mine[p] = one * root_a
                    mine[p + 1] = (a * two - b * one) * second
                    for c in range(p + 2, GRP):
                        mine[c] = mine[c] - (mine[p] * u[c][p] + mine[p + 1] * u[c][p + 1])
                times = (s * groups + g) * GRP * GRP
                for j in range(GRP):
                    times_ref[times + GRP * j : times + GRP * (j + 1), :] = mine[j]
                    rest[g] = rest[g] - mine[j] * done[j]
                for h in range(s + 1, g + 1):
                    other = (s * groups + h) * GRP * GRP
                    for c in range(GRP):
                        total = low[g][h * GRP + c]
                        for j in range(0, GRP, 2):
                            at = other + GRP * j + c
                            total = total - (
                                mine[j] * times_ref[at : at + 1, :]
                                + mine[j + 1] * times_ref[at + GRP : at + GRP + 1, :]
                            )
                        low[g][h * GRP + c] = total
        solved = row_ref[...]
        inv_ref[r0 : r0 + MIC, :] = jnp.where(lane < r0 + MIC, solved, 0.0)
        if r0 + MIC < BLK:
            high, low_part = split2(solved)
            fix = dot(
                jnp.concatenate([high, high, low_part], axis=0),
                jnp.concatenate([high, low_part, high], axis=0),
                0,
                0,
            )
            lanes = lax.broadcasted_iota(jnp.int32, (BLK - r0 - MIC, BLK), 1)
            keep = (lanes < r0) | (lanes >= r0 + MIC)
            left = jnp.where(keep, d_ref[r0 + MIC :, :], 0.0)
            d_ref[r0 + MIC :, :] = left - fix[r0 + MIC :, :]
    while queue:
        queue.pop(0)()


def factor_kernel(plan, out_rows, width, *refs):
    n, nb = plan.state_total, plan.blocks
    slots = max(plan.fan(flow, 0) for flow in range(len(plan.orders)))
    ins, (trans_ref, r_ref, z_ref, x_ref, *scratch) = refs[: slots * plan.cols], refs[slots * plan.cols :]
    (
        packed,
        d_ref,
        inv_ref,
        cast_ref,
        times_ref,
        strip_ref,
        row_ref,
        panel_ref,
        turn_ref,
        next_ref,
        full_ref,
        col_ref,
        diag_ref,
        root_ref,
        *state,
    ) = scratch
    left, right, z_all = state[:2], state[2:4], state[4]
    me, core = lax.axis_index("rows"), lax.axis_index("cols")

    for e in range(plan.cols):
        offsets = [0] * slots
        for flow in range(len(plan.orders)):
            piece, order = plan.pieces[flow], plan.orders[flow]
            inner = plan.span(flow, 0) // piece
            for d in range(plan.fan(flow, 0)):
                for f in range(inner):
                    place = plan.digit(me, order[0]) ^ d
                    rest, size = f, inner
                    for stage in order[1:]:
                        size //= plan.radix[stage]
                        place = place * plan.radix[stage] + (plan.digit(me, stage) ^ (rest // size))
                        rest %= size
                    target = (core ^ e) * plan.half + plan.base(flow) + place * piece
                    at = offsets[d] + f * piece
                    packed[pl.ds(pl.multiple_of(target, 8), piece), :] = ins[e * slots + d][
                        at : at + piece, :
                    ]
                offsets[d] += inner * piece
    full_ref[...] = jnp.zeros_like(full_ref)

    row_id = lax.broadcasted_iota(jnp.int32, (BLK, BLK), 0)
    col_id = lax.broadcasted_iota(jnp.int32, (BLK, BLK), 1)

    def turned(row):
        return jnp.broadcast_to(row, (BLK, BLK)).T

    moments = [packed[plan.extra + k : plan.extra + k + 1, :] for k in range(nb)]

    scales = []
    for k in range(0, nb, 2):
        row, spare = plan.tile(k, k), plan.diagonal_row(k + 1)
        both = packed[row : row + BLK, :]
        mirror = both.T
        second = packed[spare : spare + 1, :]
        diag_ref[k] = jnp.where(col_id >= row_id, both, mirror)
        lower = jnp.where(col_id < row_id, both, mirror)
        diag_ref[k + 1] = jnp.where(col_id == row_id, jnp.broadcast_to(second, (BLK, BLK)), lower)
        first = jnp.sum(jnp.where(row_id == col_id, both, 0.0), axis=0, keepdims=True)
        for at, diagonal in ((k, first), (k + 1, second)):
            scales.append(lax.rsqrt(diagonal))
            root_ref[at : at + 1, :] = diagonal * scales[at]
            col_ref[at] = turned(scales[at])

    def base(k, j):
        if j == k:
            return diag_ref[k] * col_ref[k] * scales[k]
        if j < nb:
            row = plan.tile(k, j)
            return packed[row : row + BLK, :] * col_ref[k] * scales[j]
        if j < nb + width // BLK:
            at = (j - nb) * BLK
            return trans_ref[at : at + BLK, k * BLK : (k + 1) * BLK].T * col_ref[k]
        return turned(moments[k] * scales[k])

    last = nb + width // BLK

    def lanes_of(tiles):
        return slice(tiles[0] * BLK, (tiles[-1] + 1) * BLK)

    def updated(k, tiles, upto=None):
        value = base(k, tiles[0])
        if len(tiles) > 1:
            value = jnp.concatenate([base(k, j) for j in tiles], axis=1)
        if upto is None:
            upto = k
        if upto:
            rows, done = slice(k * BLK, (k + 1) * BLK), slice(0, upto * BLK)
            value = value - dot3(
                [ref[rows, done] for ref in left], [ref[done, lanes_of(tiles)] for ref in right]
            )
        return value

    def prepare(k, tiles):
        value = updated(k, tiles)
        panel_ref[k % 2, :, lanes_of(tiles)] = value
        if k + 1 < nb and k + 1 in tiles:
            at = tiles.index(k + 1) * BLK
            turn_ref[...] = value[:, at : at + BLK].T

    def prepare_diagonal(k):
        next_ref[...] = updated(k, [k], k - 1)

    def start_next(k, inverse):
        rows, lanes = slice(k * BLK, (k + 1) * BLK), lanes_of([k + 1])
        high, low = split2(panel_ref[k % 2, :, lanes])
        value = dot(inverse, jnp.concatenate([high, low, high], axis=0))
        turned_high, turned_low = split2(turn_ref[...])
        mirror = dot(jnp.concatenate([turned_high, turned_low, turned_high], axis=1), inverse, 1, 1)
        straight, mirrored = split2(value), split2(mirror)
        for part in range(2):
            right[part][rows, lanes] = straight[part]
            left[part][lanes, rows] = mirrored[part]
        full_ref[rows, lanes] = value * root_ref[k + 1 : k + 2, :]
        diagonal = next_ref[...] - dot3(mirrored, straight)
        d_ref[...] = diagonal
        panel_ref[(k + 1) % 2, :, lanes] = diagonal

    z_tile = [None]

    def finish(k, tiles, inverse):
        rows, lanes = slice(k * BLK, (k + 1) * BLK), lanes_of(tiles)
        high, low = split2(panel_ref[k % 2, :, lanes])
        value = dot(inverse, jnp.concatenate([high, low, high], axis=0))
        if k + 1 < nb and tiles[0] > k:
            high, low = split2(value)
            right[0][rows, lanes] = high
            right[1][rows, lanes] = low
        for at, j in enumerate(tiles):
            one = value[:, at * BLK : (at + 1) * BLK]
            if j < nb:
                kept = one * root_ref[j : j + 1, :]
                if j == k:
                    kept = jnp.where(col_id >= row_id, kept, 0.0)
                else:
                    high, low = split2(one.T)
                    left[0][j * BLK : (j + 1) * BLK, rows] = high
                    left[1][j * BLK : (j + 1) * BLK, rows] = low
                full_ref[rows, j * BLK : (j + 1) * BLK] = kept
            elif j < last:
                at_x = (j - nb) * BLK
                part_x = jnp.sum(one * z_tile[0], axis=0, keepdims=True)
                if k:
                    part_x = part_x + x_ref[:, at_x : at_x + BLK]
                x_ref[:, at_x : at_x + BLK] = part_x
            else:
                z_tile[0] = one
                z_all[:, rows] = one.T[0:1, :]

    def groups(first_tile):
        found = [[last]]
        at = first_tile
        while at < last:
            size = 1 if at % 2 or at + 1 >= last or (at < nb <= at + 1) else 2
            found.append(list(range(at, at + size)))
            at += size
        return found

    queue = []
    d_ref[...] = base(0, 0)
    panel_ref[0, :, 0:BLK] = d_ref[...]
    for k in range(nb):
        queue += [functools.partial(prepare, k, tiles) for tiles in groups(k + 1)]
        if k + 1 < nb:
            queue.append(functools.partial(prepare_diagonal, k + 1))
        factor_block(d_ref, inv_ref, cast_ref, times_ref, strip_ref, row_ref, queue)
        inv_high, inv_low = split2(inv_ref[...])
        inverse = jnp.concatenate([inv_high, inv_high, inv_low], axis=1)
        if k + 1 < nb:
            start_next(k, inverse)
        queue += [functools.partial(finish, k, tiles, inverse) for tiles in groups(min(k + 2, nb))]
        queue.append(functools.partial(finish, k, [k], inverse))
    while queue:
        queue.pop(0)()

    rows = pl.ds(pl.multiple_of(me * out_rows, 8), out_rows)
    lanes = pl.ds(pl.multiple_of(core * width, BLK), width)
    r_ref[...] = full_ref[rows, lanes]
    z_ref[...] = z_all[:, lanes]


def per_device(
    whitening,
    sensor_states,
    sensor_coefficients,
    sensor_readings,
    conduit_endpoints,
    conductance,
    balance_right_side,
    prior_root_factor,
    prior_information,
    transition,
):
    n = prior_root_factor.shape[1]
    rows, cols = lax.axis_size("rows"), lax.axis_size("cols")
    plan = Plan(n, rows, cols)
    radix = plan.radix
    params = pltpu.CompilerParams(vmem_limit_bytes=VMEM_LIMIT)
    block_rows, bal_rows = whitening.shape[0], conductance.shape[0]
    depth = block_rows + bal_rows + BLK
    hbm = pl.BlockSpec(memory_space=pltpu.HBM)
    vmem = pl.BlockSpec(memory_space=pltpu.VMEM)

    def typed(*shape):
        return jax.ShapeDtypeStruct(shape, F32)

    inputs = (
        whitening,
        sensor_states.T,
        sensor_coefficients.T,
        sensor_readings.reshape(-1, BLK),
        conduit_endpoints.T,
        conductance[None, :],
        balance_right_side[None, :],
        prior_root_factor,
        prior_information[None, :],
    )
    parts = pl.pallas_call(
        functools.partial(assemble_kernel, plan),
        out_shape=[typed(plan.span(f, 0), BLK) for f in range(len(plan.orders)) for _ in range(plan.fan(f, 0))],
        in_specs=[hbm] * len(inputs),
        out_specs=[vmem] * sum(plan.fan(f, 0) for f in range(len(plan.orders))),
        scratch_shapes=[pltpu.VMEM(x.shape, x.dtype) for x in inputs]
        + [
            pltpu.VMEM((n + 16, block_rows), BF16),
            pltpu.VMEM((n + 16, block_rows), BF16),
            pltpu.VMEM((n + 16, depth), BF16),
            pltpu.VMEM((n + 16, depth), BF16),
            pltpu.VMEM((BLK, n), F32),
            pltpu.VMEM((plan.half, BLK), F32),
            pltpu.SemaphoreType.DMA((len(inputs),)),
        ],
        compiler_params=pltpu.CompilerParams(vmem_limit_bytes=WHOLE_VMEM),
        name="assemble",
    )(*inputs)

    def exchange(stage, rel, block):
        flip = rel * plan.stride[stage]
        return lax.ppermute(block, "rows", [(i, i ^ flip) for i in range(rows)])

    steps = len(radix)
    for step in range(steps):
        parts = list(parts)
        got = []
        for flow in range(len(plan.orders)):
            fan, stage = plan.fan(flow, step), plan.orders[flow][step]
            mine = [parts.pop(0) for _ in range(fan)]
            got += mine[:1] + [exchange(stage, d, mine[d]) for d in range(1, fan)]
        last = step + 1 == steps
        shapes = [
            typed(plan.span(flow, step + 1), BLK)
            for flow in range(len(plan.orders))
            for _ in range(1 if last else plan.fan(flow, step + 1))
        ]
        parts = pl.pallas_call(
            functools.partial(sum_kernel, plan, step),
            out_shape=shapes,
            compiler_params=params,
            name="partial_sums",
        )(*got)
    blocks = list(parts)
    for step in reversed(range(steps)):
        got = []
        for flow in range(len(plan.orders)):
            fan, stage = plan.fan(flow, step), plan.orders[flow][step]
            got.append([blocks[flow]] + [exchange(stage, d, blocks[flow]) for d in range(1, fan)])
        if step:
            blocks = [jnp.concatenate(found, axis=0) for found in got]
    swap = [(i, i ^ 1) for i in range(cols)]
    (joined,) = got
    both = joined + [lax.ppermute(block, "cols", swap) for block in joined]

    width = n // cols
    out_rows = n // rows
    wide = n + width + BLK
    r_post, z_post, x_next = pl.pallas_call(
        functools.partial(factor_kernel, plan, out_rows, width),
        out_shape=[typed(out_rows, width), typed(1, width), typed(1, width)],
        in_specs=[vmem] * (len(both) + 1),
        out_specs=[vmem] * 3,
        scratch_shapes=[
            pltpu.VMEM((cols * plan.half, BLK), F32),
            pltpu.VMEM((BLK, BLK), F32),
            pltpu.VMEM((BLK, BLK), F32),
            pltpu.VMEM((MIC * GRP, BLK), F32),
            pltpu.VMEM((MIC * MIC, BLK), F32),
            pltpu.VMEM((MIC, BLK), F32),
            pltpu.VMEM((MIC, BLK), F32),
            pltpu.VMEM((2, BLK, wide), F32),
            pltpu.VMEM((BLK, BLK), F32),
            pltpu.VMEM((BLK, BLK), F32),
            pltpu.VMEM((n, n), F32),
            pltpu.VMEM((plan.blocks, BLK, BLK), F32),
            pltpu.VMEM((plan.blocks, BLK, BLK), F32),
            pltpu.VMEM((plan.blocks, BLK), F32),
            pltpu.VMEM((n, n), BF16),
            pltpu.VMEM((n, n), BF16),
            pltpu.VMEM((n, wide), BF16),
            pltpu.VMEM((n, wide), BF16),
            pltpu.VMEM((1, n), F32),
        ],
        compiler_params=params,
        name="factor",
    )(*both, transition)
    return (r_post, z_post[0], x_next[0])


def solution(mesh):
    in_specs = (
        P("rows", None),
        P("rows", None),
        P("rows", None),
        P("rows"),
        P("rows", None),
        P("rows"),
        P("rows"),
        P("rows", None),
        P("rows"),
        P("cols", None),
    )
    out_specs = (P("rows", "cols"), P("cols"), P("cols"))
    return jax.shard_map(
        per_device, mesh=mesh, in_specs=in_specs, out_specs=out_specs, check_vma=False
    )
```
